512 devices in a mesh: section: 32 (over z, core), row: 16 (over y, x).
Axes of the slice: x: 4, y: 4, z: 16, core: 2. Of those that a mesh axis runs over, the one named last changes fastest.
Arguments:
- section_inputs: bfloat16 [32, 2048, 2048], P('section', 'row'), may hold values from -6 to 6
- fresh_group: bfloat16 [2048, 2048], P('row'), may hold values from -6 to 6
- resident_state: float32 [32, 8, 128, 128], P('section'), may hold values from -162.9174 to 162.9174
- qkv_weight: bfloat16 [32, 2048, 3072], P('section', 'row'), may hold values from -0.125 to 0.125
- out_weight: bfloat16 [32, 1024, 2048], P('section', 'row'), may hold values from -0.1875 to 0.1875
- input_gain: float32 [32, 2048], P('section'), may hold values from 0.1 to 1.9
- head_gain: float32 [32, 1024], P('section'), may hold values from 0.1 to 1.9
Outputs:
- section_outputs: bfloat16 [32, 2048, 2048], P('section', 'row')
- final_state: float32 [32, 8, 128, 128], P('section')
The draws below stay inside these ranges and needn't reach their ends.
All inputs are finite; a program needn't handle non-finite values.
Results may differ from the reference program's by a relative error of at most 0.01.
Values may be sent and summed in bfloat16 or wider, within the bound.
A program may use at most 64 MiB of HBM per device.

```python
import jax
import jax.numpy as jnp
from jax import lax

D = 2048
HEADS = 8
HEAD = 128
ROWS_DEV = 128
SECTIONS = 32
GROUP = 2048
N_ROW = 16


def steps_of(key, extent, split, least, top_value):
    def one(position, shards_of):
        steps = jax.random.uniform(jax.random.fold_in(jax.random.fold_in(key, 6), position), (shards_of,), jnp.float32, least / len(split), top_value / len(split))
        return jnp.repeat(jnp.exp(steps), extent[position] // shards_of).reshape((-1,) + (1,) * (len(extent) - position - 1))

    level = one(*split[0])
    for cut in split[1:]:
        level = level * one(*cut)
    return level


def scatter_about(own_key, shape, scale, bound, cuts=(), held_as=jnp.bfloat16):
    array = scale * jax.random.normal(own_key, shape, jnp.float32)
    if cuts:
        array = array * steps_of(own_key, shape, cuts, -0.22, 0.18)
    return jnp.clip(array, -bound, bound).astype(held_as)


def setup_inputs(seed: int = 0) -> dict:
    splits = jax.random.split(jax.random.key(seed), 8)
    return {
        "section_inputs": scatter_about(splits[0], (SECTIONS, GROUP, D), 1.0, 6.0, ((0, 32), (1, 16))),
        "fresh_group": scatter_about(splits[1], (GROUP, D), 1.0, 6.0, ((0, 16),)),
        "resident_state": scatter_about(splits[2], (SECTIONS, HEADS, HEAD, HEAD), (0.6 * (ROWS_DEV * N_ROW) ** 0.5), 162.9174, ((0, 32),), jnp.float32),
        "qkv_weight": scatter_about(splits[3], (SECTIONS, D, 3 * HEADS * HEAD), D ** -0.5, 0.125, ((0, 32), (1, 16))),
        "out_weight": scatter_about(splits[4], (SECTIONS, HEADS * HEAD, D), (HEADS * HEAD) ** -0.5, 0.1875, ((0, 32), (1, 16))),
        "input_gain": jnp.clip(1.0 + 0.18 * jax.random.normal(splits[5], (SECTIONS, D), jnp.float32), 0.1, 1.9),
        "head_gain": jnp.clip(1.0 + 0.18 * jax.random.normal(splits[6], (SECTIONS, HEADS * HEAD), jnp.float32), 0.1, 1.9),
    }


def layer(inputs, state, qkv_weight, out_weight, input_gain, head_gain):
    width = HEADS * HEAD
    highest = lax.Precision.HIGHEST
    wide = inputs.astype(jnp.float32)
    normed = (wide * lax.rsqrt(lax.optimization_barrier(jnp.mean(wide * wide, axis=-1, keepdims=True)) + 1e-05) * input_gain).astype(jnp.bfloat16)
    projected = jnp.dot(normed, qkv_weight, preferred_element_type=jnp.float32)
    queries = jax.nn.silu(projected[:, :width]).astype(jnp.bfloat16)
    key_rows = jax.nn.silu(projected[:, width:2 * width]).astype(jnp.bfloat16)
    value_rows = projected[:, 2 * width:].astype(jnp.bfloat16)
    shape = (N_ROW, ROWS_DEV, HEADS, HEAD)
    query_blocks = queries.reshape(shape).astype(jnp.float32)
    key_blocks = key_rows.reshape(shape).astype(jnp.float32)
    value_blocks = value_rows.reshape(shape).astype(jnp.float32)
    block_state = jnp.einsum('bjhd,bjhe->bhde', key_blocks, value_blocks, precision=highest)
    running = jnp.cumsum(block_state, axis=0)
    before = jnp.concatenate([jnp.zeros_like(block_state[:1]), running[:-1]], axis=0)
    prefix = state[None] + before
    carried = jnp.einsum('bihd,bhde->bihe', query_blocks, prefix, precision=highest)
    scores = jnp.einsum('bihd,bjhd->bhij', query_blocks, key_blocks, precision=highest)
    causal = jnp.tril(jnp.ones((ROWS_DEV, ROWS_DEV), dtype=bool))
    weights = jnp.where(causal, scores, 0.0).astype(jnp.bfloat16)
    weights_back = lax.optimization_barrier(weights).astype(jnp.float32)
    local = jnp.einsum('bhij,bjhe->bihe', weights_back, value_blocks, precision=highest)
    attended = (carried + local).reshape(N_ROW * ROWS_DEV, HEADS, HEAD)
    scaled = attended * lax.rsqrt(lax.optimization_barrier(jnp.mean(attended * attended, axis=-1, keepdims=True)) + 1e-06)
    head_out = (scaled.reshape(N_ROW * ROWS_DEV, width) * head_gain).astype(jnp.bfloat16)
    result = (wide + jnp.dot(head_out, out_weight, preferred_element_type=jnp.float32)).astype(jnp.bfloat16)
    return (result, state + lax.optimization_barrier(jnp.sum(block_state, axis=0)))

def one_section(packed):
    return layer(*packed)

def reference(section_inputs, fresh_group, resident_state, qkv_weight, out_weight, input_gain, head_gain):
    first_out, first_state = lax.map(one_section, (section_inputs, resident_state, qkv_weight, out_weight, input_gain, head_gain))
    second_in = jnp.concatenate([fresh_group[None], first_out[:-1]], axis=0)
    section_outputs, final_state = lax.map(one_section, (second_in, first_state, qkv_weight, out_weight, input_gain, head_gain))
    return (section_outputs, final_state)
```

```python
import functools

import jax
import jax.numpy as jnp
from jax import lax
from jax.experimental import pallas as pl
from jax.experimental.pallas import tpu as pltpu
from jax.sharding import PartitionSpec as P

MESH = pl.DeviceIdType.MESH
F32 = jnp.float32
BF16 = jnp.bfloat16
SIDES = (1, 3)
IDS = {}


def slot(*key):
    return IDS.setdefault(key, len(IDS))


for _d in (1, 3, 2):
    for _p in range(3):
        slot("A", _d, _p)
for _e in range(4):
    slot("B", _e, 1), slot("B", _e, 3), slot("F", _e)
for _d in SIDES:
    for _h in range(2):
        slot("C", _d, _h), slot("D", _d, _h)
        for _c in range(4):
            slot("E", _c, _d, _h)
    slot("CF", _d), slot("DF", _d)
    for _c in range(4):
        slot("EF", _c, _d)
for _b in range(4):
    for _d in SIDES:
        slot("H", _b, _d), slot("G", _b, _d)
    slot("HF", _b), slot("GF", _b), slot("Z", _b)
for _d in (1, 2, 3):
    slot("T", 0, _d), slot("T", 1, _d), slot("R", _d), slot("H2", _d), slot("S", _d)


def kernel(
    last, x_in, fresh, state_in, w_in, wo_in, gain, hgain, out, fstate,
    wb, wof, x1, x2, nb, pj, qb, kb, vb, al, pre, run, tsum, ho, ho2s, ho2, yb, st, fs,
    ss, rs, ls,
):
    s = lax.axis_index("section")
    r = lax.axis_index("row")
    y = r // 4
    x = lax.rem(r, 4)

    def xr(d):
        return lax.rem(x + d, 4)

    def yr(d):
        return lax.rem(y + d, 4)

    def dx(d):
        return (s, y * 4 + xr(d))

    def dy(d):
        return (s, yr(d) * 4 + x)

    def rows(b):
        return pl.ds(pl.multiple_of(b * 128, 128), 128)

    def cols(j, n):
        return pl.ds(pl.multiple_of(j * n, n), n)

    makers = {}

    def define(key, src, dst, dev):
        i = IDS[key]
        makers[key] = lambda: pltpu.make_async_remote_copy(
            src_ref=src, dst_ref=dst, send_sem=ss.at[i], recv_sem=rs.at[i],
            device_id=dev, device_id_type=MESH,
        )

    def start(*key):
        makers[key]().start()

    def got(*key):
        makers[key]().wait_recv()

    def sent(*key):
        makers[key]().wait_send()

    for d in (1, 3, 2):
        for p in range(3):
            define(("A", d, p), w_in.at[:, pl.ds(pl.multiple_of(p * 1024 + xr(d) * 256, 256), 256)],
                   wb.at[r, :, pl.ds(p * 256, 256)], dx(d))
    for e in range(4):
        k = y * 4 + xr(4 - e)
        for d in SIDES:
            define(("B", e, d), wb.at[k], wb.at[k], dy(d))
        fd = 1 if e in (0, 3) else 3
        k2 = yr(4 - fd) * 4 + xr(4 - e)
        define(("F", e), wb.at[k2], wb.at[k2], dy(fd))
    for d in SIDES:
        for h in range(2):
            v = x1.at[x, pl.ds(h * 64, 64)]
            define(("C", d, h), v, v, dx(d))
            v = wof.at[r, pl.ds(h * 32, 32)]
            define(("D", d, h), v, v, dx(d))
        h = 0 if d == 1 else 1
        v = x1.at[xr(4 - d), pl.ds(h * 64, 64)]
        define(("CF", d), v, v, dx(d))
        v = wof.at[y * 4 + xr(4 - d), pl.ds(h * 32, 32)]
        define(("DF", d), v, v, dx(d))
    for c in range(4):
        for d in SIDES:
            for h in range(2):
                v = wof.at[pl.ds(y * 4 + 2 * h, 2), :, cols(xr(c), 512)]
                define(("E", c, d, h), v, v, dy(d))
            h = 0 if d == 1 else 1
            v = wof.at[pl.ds(yr(4 - d) * 4 + 2 * h, 2), :, cols(xr(c), 512)]
            define(("EF", c, d), v, v, dy(d))
    for d in (1, 2, 3):
        for t in range(2):
            define(("T", t, d), tsum.at[t, y], tsum.at[t, y], dy(d))
        define(("R", d), fresh.at[:, cols(xr(d), 512)], x2.at[xr(d), rows(x)], dx(d))
        define(("H2", d), ho2s.at[rows(xr(d))], ho2.at[x], dx(d))
        define(("S", d), fs.at[pl.ds(2 * x, 2)], fs.at[pl.ds(2 * x, 2)], dx(d))
    for b in range(4):
        rb = pl.ds(b * 128, 128)
        for d in SIDES:
            v = ho.at[x, rb]
            define(("H", b, d), v, v, dx(d))
            v = x2.at[x, rb]
            define(("G", b, d), v, v, dx(d))
        fd = 1 if b % 2 == 0 else 3
        v = ho.at[xr(4 - fd), rb]
        define(("HF", b), v, v, dx(fd))
        v = x2.at[xr(4 - fd), rb]
        define(("GF", b), v, v, dx(fd))
        define(("Z", b), yb.at[rb], x2.at[x, rb], (s + 1, r))

    loads = [
        pltpu.make_async_copy(w_in.at[:, pl.ds(pl.multiple_of(p * 1024 + x * 256, 256), 256)],
                              wb.at[r, :, pl.ds(p * 256, 256)], ls.at[p])
        for p in range(3)
    ]
    loads.append(pltpu.make_async_copy(x_in, x1.at[x], ls.at[3]))
    loads.append(pltpu.make_async_copy(wo_in, wof.at[r], ls.at[4]))
    loads.append(pltpu.make_async_copy(state_in.at[pl.ds(2 * x, 2)], st, ls.at[5]))
    for c in loads:
        c.start()
    own_fresh = pltpu.make_async_copy(fresh.at[:, cols(x, 512)], x2.at[x, rows(x)], ls.at[6])

    barrier = pltpu.get_barrier_semaphore()
    before, after = (lax.rem(s + last, last + 1), r), (lax.rem(s + 1, last + 1), r)
    for dev in [dx(1), dx(2), dx(3), dy(1), dy(2), dy(3), before, after]:
        pl.semaphore_signal(barrier, inc=1, device_id=dev, device_id_type=MESH)
    pl.semaphore_wait(barrier, 8)

    def norm_first(b):
        def strip(i, carry):
            at = pl.ds(pl.multiple_of(i * 16, 16), 16)
            v = x1[b, at, :].astype(F32)
            scale = lax.rsqrt(jnp.mean(v * v, axis=-1, keepdims=True) + 1e-05)
            n = (v * scale * gain[...]).astype(BF16)
            to = pl.ds(pl.multiple_of(b * 128 + i * 16, 16), 16)
            for p in range(4):
                nb[p, to, :] = n[:, p * 512:(p + 1) * 512]
            return carry
        lax.fori_loop(0, 8, strip, 0)

    def norm_second(b):
        def strip(i, carry):
            at = pl.ds(pl.multiple_of(b * 128 + i * 16, 16), 16)
            v = [x2[p, at, :].astype(F32) for p in range(4)]
            sq = sum(jnp.sum(u * u, axis=-1, keepdims=True) for u in v)
            scale = lax.rsqrt(sq * (1.0 / 2048) + 1e-05)
            for p in range(4):
                nb[p, at, :] = (v[p] * scale * gain[:, p * 512:(p + 1) * 512]).astype(BF16)
            return carry
        lax.fori_loop(0, 8, strip, 0)

    def project_slice(kg, first):
        for n in range(3):
            at = pl.ds(n * 256, 256)
            w = wb[pl.ds(4 * kg, 4), :, at].reshape(512, 256)
            v = jnp.dot(nb[kg], w, preferred_element_type=F32)
            if first:
                pj[:, at] = v
            else:
                pj[:, at] += v

    def project_block(b):
        rb = pl.ds(b * 128, 128)
        for n in range(3):
            at = pl.ds(n * 256, 256)
            v = jnp.zeros((128, 256), F32)
            for kg in range(4):
                w = wb[pl.ds(4 * kg, 4), :, at].reshape(512, 256)
                v += jnp.dot(nb[kg, rb, :], w, preferred_element_type=F32)
            pj[rb, at] = v

    def states(b):
        rb = rows(b)
        for h in range(2):
            at = pl.ds(h * 128, 128)
            q = pj[rb, pl.ds(h * 128, 128)]
            qb[rb, at] = (q / (1.0 + jnp.exp(-q))).astype(BF16)
            k = pj[rb, pl.ds(256 + h * 128, 128)]
            k = (k / (1.0 + jnp.exp(-k))).astype(BF16)
            kb[rb, at] = k
            v = pj[rb, pl.ds(512 + h * 128, 128)].astype(BF16)
            vb[rb, at] = v
            pre[b, h] = run[h]
            run[h] += lax.dot_general(k, v, (((0,), (0,)), ((), ())), preferred_element_type=F32)

    def local(b):
        rb = rows(b)
        keep = lax.broadcasted_iota(jnp.int32, (128, 128), 0) >= lax.broadcasted_iota(jnp.int32, (128, 128), 1)
        for h in range(2):
            at = pl.ds(h * 128, 128)
            sc = lax.dot_general(qb[rb, at], kb[rb, at], (((1,), (1,)), ((), ())), preferred_element_type=F32)
            w = jnp.where(keep, sc, 0.0).astype(BF16)
            al[rb, at] = jnp.dot(w, vb[rb, at], preferred_element_type=F32)

    def send_totals(t):
        tsum[t, y] = run[...].astype(BF16)
        for d in (1, 3, 2):
            start("T", t, d)

    def base_of(t):
        for d in (1, 3, 2):
            got("T", t, d)
        before = st[...]
        total = st[...]
        for i in range(4):
            u = tsum[t, i].astype(F32)
            before = before + u * (y > i).astype(F32)
            total = total + u
        run[...] = before
        st[...] = total

    def finish(b, put):
        rb = rows(b)
        for h in range(2):
            at = pl.ds(h * 128, 128)
            m = (run[h] + pre[b, h]).astype(BF16)
            a = al[rb, at] + jnp.dot(qb[rb, at], m, preferred_element_type=F32)
            a = a * lax.rsqrt(jnp.mean(a * a, axis=-1, keepdims=True) + 1e-06)
            g = hgain[:, pl.ds(pl.multiple_of(x * 256 + h * 128, 128), 128)]
            put(rb, at, (a * g).astype(BF16))

    def zero_run():
        run[...] = jnp.zeros_like(run)

    def loop(f):
        def step(b, carry):
            f(b)
            return carry
        lax.fori_loop(0, 4, step, 0)

    for d in (1, 3, 2):
        for p in range(3):
            start("A", d, p)
    for c in loads[:3]:
        c.wait()
    for d in SIDES:
        start("B", 0, d)
    loads[3].wait()
    norm_first(x)
    for e in (1, 3):
        for p in range(3):
            got("A", e, p)
        for d in SIDES:
            start("B", e, d)
    for d, h in ((1, 0), (3, 1), (1, 1), (3, 0)):
        start("C", d, h)
    for p in range(3):
        got("A", 2, p)
    for d in SIDES:
        start("B", 2, d)

    def forward_w(e):
        fd = 1 if e in (0, 3) else 3
        got("B", e, fd)
        start("F", e)

    forward_w(0)
    forward_w(1)
    got("C", 1, 0)
    start("CF", 1)
    got("C", 3, 1)
    start("CF", 3)
    loads[4].wait()
    for d, h in ((1, 0), (3, 1), (1, 1), (3, 0)):
        start("D", d, h)
    forward_w(3)
    forward_w(2)
    got("C", 1, 1)
    norm_first(xr(3))
    got("C", 3, 0)
    norm_first(xr(1))
    for e in range(4):
        got("B", e, 3 if e in (0, 3) else 1)
    got("D", 1, 0)
    start("DF", 1)
    got("D", 3, 1)
    start("DF", 3)

    @pl.when(s == 0)
    def _():
        own_fresh.start()
        for d in (1, 3, 2):
            start("R", d)

    got("CF", 1)
    got("CF", 3)
    norm_first(xr(2))
    project_slice(y, True)
    project_slice(yr(3), False)
    project_slice(yr(1), False)
    for e in range(4):
        got("F", e)
    project_slice(yr(2), False)

    zero_run()
    loop(states)
    send_totals(0)
    got("D", 1, 1)
    got("D", 3, 0)
    got("DF", 1)
    got("DF", 3)
    for d, h in ((1, 0), (3, 1), (1, 1), (3, 0)):
        start("E", 0, d, h)
    loop(local)
    loads[5].wait()
    base_of(0)

    def put_first(rb, at, v):
        ho[x, rb, at] = v

    for b in range(4):
        finish(b, put_first)
        for d in SIDES:
            start("H", b, d)
    got("E", 0, 1, 0)
    start("EF", 0, 1)
    got("E", 0, 3, 1)
    start("EF", 0, 3)
    got("E", 0, 1, 1)
    got("E", 0, 3, 0)
    for c in range(1, 4):
        for d, h in ((1, 0), (3, 1), (1, 1), (3, 0)):
            start("E", c, d, h)

    def forward_h(b):
        got("H", b, 1)
        got("H", b, 3)
        start("HF", b)

    def out_first(b):
        got("HF", b)
        rb = pl.ds(b * 128, 128)
        for n in range(2):
            at = pl.ds(pl.multiple_of(x * 512 + n * 256, 256), 256)
            v = x1[b, :, at].astype(F32)
            for j in range(4):
                w = wof[pl.ds(4 * j, 4), :, at].reshape(256, 256)
                v += jnp.dot(ho[j, rb, :], w, preferred_element_type=F32)
            yb[rb, pl.ds(n * 256, 256)] = v.astype(BF16)

        @pl.when(s < last)
        def _():
            start("Z", b)

    def gather_second(b):
        @pl.when(s > 0)
        def _():
            got("Z", b)

        for d in SIDES:
            start("G", b, d)

    def forward_g(b):
        got("G", b, 1)
        got("G", b, 3)
        start("GF", b)

    def second(b):
        got("GF", b)
        norm_second(b)
        project_block(b)
        states(b)

    @pl.when(s == 0)
    def _():
        own_fresh.wait()
        for d in (1, 3, 2):
            got("R", d)

    forward_h(0)
    forward_h(1)
    got("EF", 0, 1)
    got("EF", 0, 3)
    out_first(0)
    forward_h(2)
    out_first(1)
    gather_second(0)
    forward_h(3)
    out_first(2)
    gather_second(1)
    out_first(3)
    forward_g(0)
    gather_second(2)
    gather_second(3)
    for c in range(1, 4):
        got("E", c, 1, 0)
        start("EF", c, 1)
        got("E", c, 3, 1)
        start("EF", c, 3)
    forward_g(1)
    zero_run()
    second(0)
    forward_g(2)
    second(1)
    forward_g(3)
    second(2)
    second(3)

    send_totals(1)
    loop(local)
    base_of(1)
    fs[pl.ds(2 * x, 2)] = st[...].astype(BF16)

    def put_second(rb, at, v):
        ho2s[rb, at] = v

    for d in (2, 1, 3):
        finish(xr(d), put_second)
        start("H2", d)
    for d in (2, 1, 3):
        start("S", d)

    def put_own(rb, at, v):
        ho2[x, :, at] = v

    finish(x, put_own)
    for c in range(1, 4):
        got("E", c, 1, 1)
        got("E", c, 3, 0)
        got("EF", c, 1)
        got("EF", c, 3)
    for d in (1, 3, 2):
        got("H2", d)
    for n in range(8):
        at = pl.ds(n * 256, 256)
        v = x2[n // 2, rows(x), pl.ds((n % 2) * 256, 256)].astype(F32)
        for j in range(4):
            w = wof[pl.ds(4 * j, 4), :, at].reshape(256, 256)
            v += jnp.dot(ho2[j], w, preferred_element_type=F32)
        out[:, at] = v.astype(BF16)
    for d in (1, 3, 2):
        got("S", d)
    fstate[...] = fs[...].astype(F32)

    for key in IDS:
        if key[0] == "Z":
            @pl.when(s < last)
            def _():
                sent(*key)
        elif key[0] == "R":
            @pl.when(s == 0)
            def _():
                sent(*key)
        else:
            sent(*key)


def body(section_inputs, fresh_group, resident_state, qkv_weight, out_weight, input_gain, head_gain):
    anywhere = pl.BlockSpec(memory_space=pl.ANY)
    vmem = pl.BlockSpec(memory_space=pltpu.VMEM)
    n = len(IDS)
    out, state = pl.pallas_call(
        functools.partial(kernel, lax.axis_size("section") - 1),
        name="two_ticks",
        out_shape=(
            jax.ShapeDtypeStruct((128, 2048), BF16),
            jax.ShapeDtypeStruct((8, 128, 128), F32),
        ),
        in_specs=[anywhere] * 5 + [vmem] * 2,
        out_specs=(vmem, vmem),
        scratch_shapes=[
            pltpu.VMEM((16, 128, 768), BF16),
            pltpu.VMEM((16, 64, 2048), BF16),
            pltpu.VMEM((4, 128, 2048), BF16),
            pltpu.VMEM((4, 512, 512), BF16),
            pltpu.VMEM((4, 512, 512), BF16),
            pltpu.VMEM((512, 768), F32),
            pltpu.VMEM((512, 256), BF16),
            pltpu.VMEM((512, 256), BF16),
            pltpu.VMEM((512, 256), BF16),
            pltpu.VMEM((512, 256), F32),
            pltpu.VMEM((4, 2, 128, 128), F32),
            pltpu.VMEM((2, 128, 128), F32),
            pltpu.VMEM((2, 4, 2, 128, 128), BF16),
            pltpu.VMEM((4, 512, 256), BF16),
            pltpu.VMEM((512, 256), BF16),
            pltpu.VMEM((4, 128, 256), BF16),
            pltpu.VMEM((512, 512), BF16),
            pltpu.VMEM((2, 128, 128), F32),
            pltpu.VMEM((8, 128, 128), BF16),
            pltpu.SemaphoreType.DMA((n,)),
            pltpu.SemaphoreType.DMA((n,)),
            pltpu.SemaphoreType.DMA((7,)),
        ],
        compiler_params=pltpu.CompilerParams(
            collective_id=0, has_side_effects=True, vmem_limit_bytes=48 * 2**20
        ),
        cost_estimate=pl.CostEstimate(flops=4_600_000_000, bytes_accessed=4_000_000, transcendentals=0),
    )(
        section_inputs[0], fresh_group, resident_state[0], qkv_weight[0], out_weight[0], input_gain, head_gain
    )
    return (out[None], state[None])


def solution(mesh):
    in_specs = (
        P("section", "row", None),
        P("row", None),
        P("section", None, None, None),
        P("section", "row", None),
        P("section", "row", None),
        P("section", None),
        P("section", None),
    )
    out_specs = (P("section", "row", None), P("section", None, None, None))
    return jax.shard_map(body, mesh=mesh, in_specs=in_specs, out_specs=out_specs, check_vma=False)
```

```python
import functools

import jax
import jax.numpy as jnp
from jax import lax
from jax.experimental import pallas as pl
from jax.experimental.pallas import tpu as pltpu
from jax.sharding import PartitionSpec as P

MESH = pl.DeviceIdType.MESH
F32 = jnp.float32
BF16 = jnp.bfloat16
SIDES = (1, 3)
OTHERS = (1, 3, 2)
STAGES = 2
PART = 128 // STAGES
IDS = {}


def slot(*key):
    return IDS.setdefault(key, len(IDS))


for _d in OTHERS:
    for _p in range(3):
        slot("A", _d, _p)
    slot("D", _d), slot("S", _d), slot("T", 0, _d), slot("T", 1, _d)
slot("X")
for _e in range(4):
    for _d in SIDES:
        slot("B", _e, _d), slot("E", _e, _d)
    slot("F", _e), slot("EF", _e)
for _d in SIDES:
    for _h in range(2):
        slot("C", _d, _h)
    slot("CF", _d)
for _q in range(STAGES):
    for _t in range(2):
        for _d in SIDES:
            slot("H", _t, _q, _d)
        slot("HF", _t, _q)
    for _d in SIDES:
        slot("G", _q, _d)
    slot("GF", _q)
    for _d in range(4):
        slot("Z", _q, _d), slot("O", _q, _d)


def kernel(
    last, x_in, fresh, state_in, w_in, wo_in, gain_in, hgain_in, out, fstate,
    wb, wos, x1, x2, nb, pj, qb, kb, vb, al, pre, run, tsum, ho, yb, st, gain, hgain,
    ss, rs, ls,
):
    s = lax.axis_index("section")
    r = lax.axis_index("row")
    odd = lax.rem(s, 2)
    py = r // 4
    px = lax.rem(r, 4)
    g = py + odd * (px - py)
    u = px + odd * (py - px)

    def ur(d):
        return lax.rem(u + d, 4)

    def gr(d):
        return lax.rem(g + d, 4)

    def row_of(gg, uu):
        return gg * (4 - 3 * odd) + uu * (1 + 3 * odd)

    def row_of_next(gg, uu):
        return gg * (1 + 3 * odd) + uu * (4 - 3 * odd)

    def du(d):
        return (s, row_of(g, ur(d)))

    def dg(d):
        return (s, row_of(gr(d), u))

    def cols(j, n):
        return pl.ds(pl.multiple_of(j * n, n), n)

    def part(q):
        return pl.ds(q * PART, PART)

    before = lax.rem(s + last, last + 1)
    after = lax.rem(s + 1, last + 1)
    makers = {}

    def define(key, src, dst, dev):
        i = IDS[key]
        makers[key] = lambda: pltpu.make_async_remote_copy(
            src_ref=src, dst_ref=dst, send_sem=ss.at[i], recv_sem=rs.at[i],
            device_id=dev, device_id_type=MESH,
        )

    def start(*key):
        makers[key]().start()

    def got(*key):
        makers[key]().wait_recv()

    def sent(*key):
        makers[key]().wait_send()

    for d in OTHERS:
        for p in range(3):
            define(("A", d, p), w_in.at[:, pl.ds(pl.multiple_of(p * 1024 + ur(d) * 256, 256), 256)],
                   wb.at[g, u, :, pl.ds(p * 256, 256)], du(d))
        define(("D", d), wo_in.at[:, cols(ur(d), 512)], wos.at[r], du(d))
        for t in range(2):
            define(("T", t, d), tsum.at[t, g], tsum.at[t, g], dg(d))
        v = fstate.at[pl.ds(2 * u, 2)]
        define(("S", d), v, v, du(d))
    for e in range(4):
        src = ur(4 - e)
        fd = 1 if e in (0, 3) else 3
        for d in SIDES:
            v = wb.at[g, src]
            define(("B", e, d), v, v, dg(d))
            v = wos.at[row_of(g, src)]
            define(("E", e, d), v, v, dg(d))
        v = wb.at[gr(4 - fd), src]
        define(("F", e), v, v, dg(fd))
        v = wos.at[row_of(gr(4 - fd), src)]
        define(("EF", e), v, v, dg(fd))
    for d in SIDES:
        for h in range(2):
            v = x1.at[u, pl.ds(h * 64, 64)]
            define(("C", d, h), v, v, du(d))
        v = x1.at[ur(4 - d), pl.ds((0 if d == 1 else 1) * 64, 64)]
        define(("CF", d), v, v, du(d))
    for q in range(STAGES):
        fd = SIDES[q % 2]
        for t in range(2):
            for d in SIDES:
                v = ho.at[t, u, :, part(q)]
                define(("H", t, q, d), v, v, du(d))
            v = ho.at[t, ur(4 - fd), :, part(q)]
            define(("HF", t, q), v, v, du(fd))
        for d in SIDES:
            v = x2.at[u, part(q)]
            define(("G", q, d), v, v, du(d))
        v = x2.at[ur(4 - fd), part(q)]
        define(("GF", q), v, v, du(fd))
        for d in range(4):
            define(("Z", q, d), yb.at[0, ur(d), part(q)], x2.at[ur(d), part(q), cols(u, 512)],
                   (after, row_of_next(g, ur(d))))
            define(("O", q, d), yb.at[1, ur(d), part(q)], out.at[part(q), cols(u, 512)], (s, 4 * g + ur(d)))
    apart = odd * (g - u) != 0
    here = odd * (g - u) == 0
    define(("X",), x_in, x1.at[g], (s, 4 * g + u))

    loads = [
        pltpu.make_async_copy(w_in.at[:, pl.ds(pl.multiple_of(p * 1024 + u * 256, 256), 256)],
                              wb.at[g, u, :, pl.ds(p * 256, 256)], ls.at[p])
        for p in range(3)
    ]
    own_block = pltpu.make_async_copy(x_in, x1.at[u], ls.at[3])
    loads.append(pltpu.make_async_copy(wo_in.at[:, cols(u, 512)], wos.at[r], ls.at[4]))
    loads.append(pltpu.make_async_copy(state_in.at[pl.ds(2 * u, 2)], st, ls.at[5]))
    loads.append(pltpu.make_async_copy(gain_in, gain, ls.at[6]))
    loads.append(pltpu.make_async_copy(hgain_in, hgain, ls.at[7]))
    own_fresh = pltpu.make_async_copy(fresh, x2.at[u], ls.at[8])
    for c in loads:
        c.start()

    @pl.when(here)
    def _():
        own_block.start()

    @pl.when(s == 0)
    def _():
        own_fresh.start()

    barrier = pltpu.get_barrier_semaphore()
    for dev in [(s, lax.rem(r + d, 16)) for d in range(1, 16)] + [(before, row_of_next(g, ur(d))) for d in range(4)]:
        pl.semaphore_signal(barrier, inc=1, device_id=dev, device_id_type=MESH)
    pl.semaphore_wait(barrier, 19)

    def norm(xs, b, low, count):
        def strip(i, carry):
            at = pl.ds(pl.multiple_of(low + i * 16, 16), 16)
            v = xs[b, at, :].astype(F32)
            v = v * lax.rsqrt(jnp.mean(v * v, axis=-1, keepdims=True) + 1e-05)
            for k in range(16):
                g2 = k // 4 + odd * (k % 4 - k // 4)
                u2 = k % 4 + odd * (k // 4 - k % 4)
                ks = slice(k * 128, k * 128 + 128)
                nb[g2, b, at, cols(u2, 128)] = (v[:, ks] * gain[:, ks]).astype(BF16)
            return carry
        lax.fori_loop(0, count // 16, strip, 0, unroll=4)

    def keep_projected(n, v, at):
        if n < 2:
            v = v / (1.0 + jnp.exp(-v))
        [qb, kb, vb][n][:, at, :] = v.astype(BF16).reshape(4, -1, 256)

    def project_slice(g2, first=False, final=False):
        def one(i, carry):
            at = pl.ds(pl.multiple_of(i * 64, 64), 64)
            for n in range(3):
                to = pl.ds(n * 256, 256)
                w = wb[g2, :, :, to].reshape(512, 256)
                v = jnp.dot(nb[g2, :, at].reshape(256, 512), w, preferred_element_type=F32)
                if not first:
                    v += pj[:, at, to].reshape(256, 256)
                if final:
                    keep_projected(n, v, at)
                else:
                    pj[:, at, to] = v.reshape(4, 64, 256)
            return carry
        lax.fori_loop(0, 2, one, 0)

    def project_stage(q):
        for n in range(3):
            to = pl.ds(n * 256, 256)
            v = jnp.zeros((4 * PART, 256), F32)
            for g2 in range(4):
                w = wb[g2, :, :, to].reshape(512, 256)
                v += jnp.dot(nb[g2, :, part(q)].reshape(4 * PART, 512), w, preferred_element_type=F32)
            keep_projected(n, v, part(q))

    def states(t):
        for h in range(2):
            at = pl.ds(h * 128, 128)
            total = jnp.zeros((128, 128), F32)
            for b in range(4):
                pre[b, h] = total
                total += lax.dot_general(
                    kb[b, :, at], vb[b, :, at], (((0,), (0,)), ((), ())), preferred_element_type=F32
                )
            tsum[t, g, h] = total.astype(BF16)
        for d in OTHERS:
            start("T", t, d)

    def local():
        keep = lax.broadcasted_iota(jnp.int32, (128, 128), 0) >= lax.broadcasted_iota(jnp.int32, (128, 128), 1)
        for b in range(4):
            for h in range(2):
                at = pl.ds(h * 128, 128)
                sc = lax.dot_general(qb[b, :, at], kb[b, :, at], (((1,), (1,)), ((), ())), preferred_element_type=F32)
                w = jnp.where(keep, sc, 0.0).astype(BF16)
                al[b, :, at] = jnp.dot(w, vb[b, :, at], preferred_element_type=F32)

    def prefixes(t):
        for d in OTHERS:
            got("T", t, d)
        for h in range(2):
            ahead = st[h]
            whole = ahead
            for j in range(4):
                v = tsum[t, j, h].astype(F32)
                ahead = ahead + v * (j < g).astype(F32)
                whole = whole + v
            run[h] = ahead
            st[h] = whole

    def finish(t):
        for b in range(4):
            for h in range(2):
                at = pl.ds(h * 128, 128)
                m = (run[h] + pre[b, h]).astype(BF16)
                a = al[b, :, at] + jnp.dot(qb[b, :, at], m, preferred_element_type=F32)
                a = a * lax.rsqrt(jnp.mean(a * a, axis=-1, keepdims=True) + 1e-06)
                w = hgain[:, pl.ds(pl.multiple_of(u * 256 + h * 128, 128), 128)]
                ho[t, u, b, :, at] = (a * w).astype(BF16)
        for q in range(STAGES):
            for d in SIDES:
                start("H", t, q, d)

    def forward_h(t, q):
        for d in SIDES:
            got("H", t, q, d)
        start("HF", t, q)

    def project_out(t, xs, q):
        got("HF", t, q)
        for n in range(2):
            at = pl.ds(n * 256, 256)
            v = xs[:, part(q), pl.ds(pl.multiple_of(u * 512 + n * 256, 256), 256)].astype(F32).reshape(4 * PART, 256)
            for j in range(4):
                w = wos[4 * j:4 * j + 4, :, at].reshape(256, 256)
                v += jnp.dot(ho[t, j, :, part(q)].reshape(4 * PART, 256), w, preferred_element_type=F32)
            yb[t, :, part(q), at] = v.astype(BF16).reshape(4, PART, 256)

    for d in OTHERS:
        for p in range(3):
            start("A", d, p)

    @pl.when(apart)
    def _():
        start("X")

    for c in loads[:3]:
        c.wait()
    for d in SIDES:
        start("B", 0, d)
    loads[5].wait()
    for e in (1, 3):
        for p in range(3):
            got("A", e, p)
        for d in SIDES:
            start("B", e, d)

    @pl.when(here)
    def _():
        own_block.wait()

    @pl.when(apart)
    def _():
        got("X")

    for d, h in ((1, 0), (3, 1), (1, 1), (3, 0)):
        start("C", d, h)
    norm(x1, u, 0, 128)
    for p in range(3):
        got("A", 2, p)
    for d in SIDES:
        start("B", 2, d)

    def forward_w(e):
        got("B", e, 1 if e in (0, 3) else 3)
        start("F", e)

    forward_w(0)
    forward_w(1)
    got("C", 1, 0)
    start("CF", 1)
    got("C", 3, 1)
    start("CF", 3)
    forward_w(3)
    forward_w(2)
    got("C", 1, 1)
    norm(x1, ur(3), 0, 128)
    got("C", 3, 0)
    norm(x1, ur(1), 0, 128)
    for d in OTHERS:
        start("D", d)
    for e in range(4):
        got("B", e, 3 if e in (0, 3) else 1)
    got("CF", 1)
    got("CF", 3)
    norm(x1, ur(2), 0, 128)
    project_slice(g, first=True)
    project_slice(gr(3))
    project_slice(gr(1))
    loads[3].wait()
    for e in (0, 1, 3, 2):
        if e:
            got("D", e)
        for d in SIDES:
            start("E", e, d)
    for e in range(4):
        got("F", e)
    project_slice(gr(2), final=True)

    states(0)
    local()

    def forward_e(e):
        got("E", e, 1 if e in (0, 3) else 3)
        start("EF", e)

    for e in (0, 1, 3, 2):
        forward_e(e)
    loads[4].wait()
    loads[6].wait()
    prefixes(0)
    finish(0)
    for q in range(STAGES):
        forward_h(0, q)
    for e in range(4):
        got("E", e, 3 if e in (0, 3) else 1)
        got("EF", e)
    for q in range(STAGES):
        project_out(0, x1, q)

        @pl.when(s < last)
        def _():
            for d in (2, 1, 3, 0):
                start("Z", q, d)

    for q in range(STAGES):
        if q == 0:
            @pl.when(s == 0)
            def _():
                own_fresh.wait()

        @pl.when(s > 0)
        def _():
            for d in range(4):
                got("Z", q, d)

        for d in SIDES:
            start("G", q, d)
    for q in range(STAGES):
        for d in SIDES:
            got("G", q, d)
        start("GF", q)
    for q in range(STAGES):
        for d in (0, 1, 3):
            norm(x2, ur(d), q * PART, PART)
        got("GF", q)
        norm(x2, ur(2), q * PART, PART)
        project_stage(q)
    states(1)
    local()
    prefixes(1)
    fstate[pl.ds(2 * u, 2)] = st[...].astype(BF16)
    for d in OTHERS:
        start("S", d)
    finish(1)
    for q in range(STAGES):
        forward_h(1, q)
    for q in range(STAGES):
        project_out(1, x2, q)
        for d in (2, 1, 3):
            start("O", q, d)

        @pl.when(apart)
        def _():
            start("O", q, 0)

    @pl.when(here)
    def _():
        out[:, cols(u, 512)] = yb[1, u]

    for q in range(STAGES):
        for d in (2, 1, 3):
            got("O", q, d)

    @pl.when(apart)
    def _():
        for q in range(STAGES):
            got("O", q, 0)

    for d in OTHERS:
        got("S", d)
    for key in IDS:
        if key[0] == "Z":
            @pl.when(s < last)
            def _():
                sent(*key)
        elif key[0] == "X" or (key[0] == "O" and key[2] == 0):
            @pl.when(apart)
            def _():
                sent(*key)
        else:
            sent(*key)


def body(section_inputs, fresh_group, resident_state, qkv_weight, out_weight, input_gain, head_gain):
    anywhere = pl.BlockSpec(memory_space=pl.ANY)
    vmem = pl.BlockSpec(memory_space=pltpu.VMEM)
    n = len(IDS)
    out, state = pl.pallas_call(
        functools.partial(kernel, lax.axis_size("section") - 1),
        name="two_ticks",
        out_shape=(
            jax.ShapeDtypeStruct((128, 2048), BF16),
            jax.ShapeDtypeStruct((8, 128, 128), BF16),
        ),
        in_specs=[anywhere] * 7,
        out_specs=(vmem, vmem),
        scratch_shapes=[
            pltpu.VMEM((4, 4, 128, 768), BF16),
            pltpu.VMEM((16, 64, 512), BF16),
            pltpu.VMEM((4, 128, 2048), BF16),
            pltpu.VMEM((4, 128, 2048), BF16),
            pltpu.VMEM((4, 4, 128, 512), BF16),
            pltpu.VMEM((4, 128, 768), F32),
            pltpu.VMEM((4, 128, 256), BF16),
            pltpu.VMEM((4, 128, 256), BF16),
            pltpu.VMEM((4, 128, 256), BF16),
            pltpu.VMEM((4, 128, 256), F32),
            pltpu.VMEM((4, 2, 128, 128), F32),
            pltpu.VMEM((2, 128, 128), F32),
            pltpu.VMEM((2, 4, 2, 128, 128), BF16),
            pltpu.VMEM((2, 4, 4, 128, 256), BF16),
            pltpu.VMEM((2, 4, 128, 512), BF16),
            pltpu.VMEM((2, 128, 128), F32),
            pltpu.VMEM((1, 2048), F32),
            pltpu.VMEM((1, 1024), F32),
            pltpu.SemaphoreType.DMA((n,)),
            pltpu.SemaphoreType.DMA((n,)),
            pltpu.SemaphoreType.DMA((9,)),
        ],
        compiler_params=pltpu.CompilerParams(
            collective_id=0, has_side_effects=True, vmem_limit_bytes=61 * 2**20
        ),
        cost_estimate=pl.CostEstimate(flops=4_600_000_000, bytes_accessed=4_000_000, transcendentals=0),
    )(
        section_inputs[0], fresh_group, resident_state[0], qkv_weight[0], out_weight[0], input_gain, head_gain
    )
    return (out[None], state.astype(F32)[None])


def solution(mesh):
    in_specs = (
        P("section", "row", None),
        P("row", None),
        P("section", None, None, None),
        P("section", "row", None),
        P("section", "row", None),
        P("section", None),
        P("section", None),
    )
    out_specs = (P("section", "row", None), P("section", None, None, None))
    return jax.shard_map(body, mesh=mesh, in_specs=in_specs, out_specs=out_specs, check_vma=False)
```

```python
import functools

import jax
import jax.numpy as jnp
from jax import lax
from jax.experimental import pallas as pl
from jax.experimental.pallas import tpu as pltpu
from jax.sharding import PartitionSpec as P

MESH = pl.DeviceIdType.MESH
F32 = jnp.float32
BF16 = jnp.bfloat16
SIDES = (1, 3)
IDS = {}


def slot(*key):
    return IDS.setdefault(key, len(IDS))


for _d in (1, 3, 2):
    for _p in range(3):
        slot("A", _d, _p)
for _e in range(4):
    slot("B", _e, 1), slot("B", _e, 3), slot("F", _e)
    slot("K", _e, 1), slot("K", _e, 3), slot("KF", _e)
for _d in SIDES:
    for _h in range(2):
        slot("C", _d, _h), slot("D", _d, _h)
        for _c in range(1, 4):
            slot("E", _c, _d, _h)
    slot("CF", _d), slot("DF", _d)
    for _c in range(1, 4):
        slot("EF", _c, _d)
for _b in range(4):
    for _d in SIDES:
        slot("H", _b, _d), slot("G", _b, _d)
    slot("HF", _b), slot("GF", _b), slot("Z", _b)
for _d in (1, 2, 3):
    slot("T", 0, _d), slot("T", 1, _d), slot("R", _d), slot("H2", _d), slot("S", _d)


def kernel(
    last, x_in, fresh, state_in, w_in, wo_in, gain_in, hgain_in, out, fstate,
    wb, wof, x1, x2, nb, pj, qb, kb, vb, al, pre, run, tsum, ho, ho2s, ho2, yb, st, gain, hgain,
    ss, rs, ls,
):
    s = lax.axis_index("section")
    r = lax.axis_index("row")
    y = r // 4
    x = lax.rem(r, 4)

    def xr(d):
        return lax.rem(x + d, 4)

    def yr(d):
        return lax.rem(y + d, 4)

    def dx(d):
        return (s, y * 4 + xr(d))

    def dy(d):
        return (s, yr(d) * 4 + x)

    def rows(b):
        return pl.ds(pl.multiple_of(b * 128, 128), 128)

    def cols(j, n):
        return pl.ds(pl.multiple_of(j * n, n), n)

    makers = {}

    def define(key, src, dst, dev):
        i = IDS[key]
        makers[key] = lambda: pltpu.make_async_remote_copy(
            src_ref=src, dst_ref=dst, send_sem=ss.at[i], recv_sem=rs.at[i],
            device_id=dev, device_id_type=MESH,
        )

    def start(*key):
        makers[key]().start()

    def got(*key):
        makers[key]().wait_recv()

    def sent(*key):
        makers[key]().wait_send()

    for d in (1, 3, 2):
        for p in range(3):
            define(("A", d, p), w_in.at[:, pl.ds(pl.multiple_of(p * 1024 + xr(d) * 256, 256), 256)],
                   wb.at[r, :, pl.ds(p * 256, 256)], dx(d))
    for e in range(4):
        k = y * 4 + xr(4 - e)
        for d in SIDES:
            define(("B", e, d), wb.at[k], wb.at[k], dy(d))
        fd = 1 if e in (0, 3) else 3
        k2 = yr(4 - fd) * 4 + xr(4 - e)
        define(("F", e), wb.at[k2], wb.at[k2], dy(fd))
        for d in SIDES:
            v = wof.at[k, :, cols(x, 512)]
            define(("K", e, d), v, v, dy(d))
        v = wof.at[k2, :, cols(x, 512)]
        define(("KF", e), v, v, dy(fd))
    for d in SIDES:
        for h in range(2):
            v = x1.at[x, pl.ds(h * 64, 64)]
            define(("C", d, h), v, v, dx(d))
            v = wof.at[r, pl.ds(h * 32, 32)]
            define(("D", d, h), v, v, dx(d))
        h = 0 if d == 1 else 1
        v = x1.at[xr(4 - d), pl.ds(h * 64, 64)]
        define(("CF", d), v, v, dx(d))
        v = wof.at[y * 4 + xr(4 - d), pl.ds(h * 32, 32)]
        define(("DF", d), v, v, dx(d))
    for c in range(1, 4):
        for d in SIDES:
            for h in range(2):
                v = wof.at[pl.ds(y * 4 + 2 * h, 2), :, cols(xr(c), 512)]
                define(("E", c, d, h), v, v, dy(d))
            h = 0 if d == 1 else 1
            v = wof.at[pl.ds(yr(4 - d) * 4 + 2 * h, 2), :, cols(xr(c), 512)]
            define(("EF", c, d), v, v, dy(d))
    for d in (1, 2, 3):
        for t in range(2):
            define(("T", t, d), tsum.at[t, y], tsum.at[t, y], dy(d))
        define(("R", d), fresh.at[:, cols(xr(d), 512)], x2.at[xr(d), rows(x)], dx(d))
        define(("H2", d), ho2s.at[rows(xr(d))], ho2.at[x], dx(d))
        define(("S", d), fstate.at[pl.ds(2 * x, 2)], fstate.at[pl.ds(2 * x, 2)], dx(d))
    for b in range(4):
        rb = pl.ds(b * 128, 128)
        for d in SIDES:
            v = ho.at[x, rb]
            define(("H", b, d), v, v, dx(d))
            v = x2.at[x, rb]
            define(("G", b, d), v, v, dx(d))
        fd = 1 if b % 2 == 0 else 3
        v = ho.at[xr(4 - fd), rb]
        define(("HF", b), v, v, dx(fd))
        v = x2.at[xr(4 - fd), rb]
        define(("GF", b), v, v, dx(fd))
        define(("Z", b), yb.at[rb], x2.at[x, rb], (s + 1, r))

    loads = [
        pltpu.make_async_copy(w_in.at[:, pl.ds(pl.multiple_of(p * 1024 + x * 256, 256), 256)],
                              wb.at[r, :, pl.ds(p * 256, 256)], ls.at[p])
        for p in range(3)
    ]
    loads.append(pltpu.make_async_copy(x_in, x1.at[x], ls.at[3]))
    loads.append(pltpu.make_async_copy(wo_in, wof.at[r], ls.at[4]))
    loads.append(pltpu.make_async_copy(state_in.at[pl.ds(2 * x, 2)], st, ls.at[5]))
    loads.append(pltpu.make_async_copy(gain_in, gain, ls.at[6]))
    loads.append(pltpu.make_async_copy(hgain_in, hgain, ls.at[7]))
    for c in loads:
        c.start()
    own_fresh = pltpu.make_async_copy(fresh.at[:, cols(x, 512)], x2.at[x, rows(x)], ls.at[8])

    barrier = pltpu.get_barrier_semaphore()
    before, after = (lax.rem(s + last, last + 1), r), (lax.rem(s + 1, last + 1), r)
    for dev in [dx(1), dx(2), dx(3), dy(1), dy(2), dy(3), before, after]:
        pl.semaphore_signal(barrier, inc=1, device_id=dev, device_id_type=MESH)
    pl.semaphore_wait(barrier, 8)

    def norm_first(b):
        def strip(i, carry):
            at = pl.ds(pl.multiple_of(i * 16, 16), 16)
            v = x1[b, at, :].astype(F32)
            scale = lax.rsqrt(jnp.mean(v * v, axis=-1, keepdims=True) + 1e-05)
            n = (v * scale * gain[...]).astype(BF16)
            to = pl.ds(pl.multiple_of(b * 128 + i * 16, 16), 16)
            for p in range(4):
                nb[p, to, :] = n[:, p * 512:(p + 1) * 512]
            return carry
        lax.fori_loop(0, 8, strip, 0, unroll=4)

    def norm_second(b):
        def strip(i, carry):
            at = pl.ds(pl.multiple_of(b * 128 + i * 16, 16), 16)
            v = [x2[p, at, :].astype(F32) for p in range(4)]
            sq = sum(jnp.sum(u * u, axis=-1, keepdims=True) for u in v)
            scale = lax.rsqrt(sq * (1.0 / 2048) + 1e-05)
            for p in range(4):
                nb[p, at, :] = (v[p] * scale * gain[:, p * 512:(p + 1) * 512]).astype(BF16)
            return carry
        lax.fori_loop(0, 8, strip, 0, unroll=4)

    def project_slice(kg, first):
        for n in range(3):
            at = pl.ds(n * 256, 256)
            w = wb[pl.ds(4 * kg, 4), :, at].reshape(512, 256)
            v = jnp.dot(nb[kg], w, preferred_element_type=F32)
            if first:
                pj[:, at] = v
            else:
                pj[:, at] += v

    def project_block(b):
        rb = pl.ds(b * 128, 128)
        for n in range(3):
            at = pl.ds(n * 256, 256)
            v = jnp.zeros((128, 256), F32)
            for kg in range(4):
                w = wb[pl.ds(4 * kg, 4), :, at].reshape(512, 256)
                v += jnp.dot(nb[kg, rb, :], w, preferred_element_type=F32)
            pj[rb, at] = v

    def states(b):
        rb = rows(b)
        for h in range(2):
            at = pl.ds(h * 128, 128)
            q = pj[rb, pl.ds(h * 128, 128)]
            qb[rb, at] = (q / (1.0 + jnp.exp(-q))).astype(BF16)
            k = pj[rb, pl.ds(256 + h * 128, 128)]
            k = (k / (1.0 + jnp.exp(-k))).astype(BF16)
            kb[rb, at] = k
            v = pj[rb, pl.ds(512 + h * 128, 128)].astype(BF16)
            vb[rb, at] = v
            pre[b, h] = run[h]
            run[h] += lax.dot_general(k, v, (((0,), (0,)), ((), ())), preferred_element_type=F32)

    def local(b):
        rb = rows(b)
        keep = lax.broadcasted_iota(jnp.int32, (128, 128), 0) >= lax.broadcasted_iota(jnp.int32, (128, 128), 1)
        for h in range(2):
            at = pl.ds(h * 128, 128)
            sc = lax.dot_general(qb[rb, at], kb[rb, at], (((1,), (1,)), ((), ())), preferred_element_type=F32)
            w = jnp.where(keep, sc, 0.0).astype(BF16)
            al[rb, at] = jnp.dot(w, vb[rb, at], preferred_element_type=F32)

    def send_totals(t):
        tsum[t, y] = run[...].astype(BF16)
        for d in (1, 3, 2):
            start("T", t, d)

    def base_of(t):
        for d in (1, 3, 2):
            got("T", t, d)
        before = st[...]
        total = st[...]
        for i in range(4):
            u = tsum[t, i].astype(F32)
            before = before + u * (y > i).astype(F32)
            total = total + u
        run[...] = before
        st[...] = total

    def finish(b, put):
        rb = rows(b)
        for h in range(2):
            at = pl.ds(h * 128, 128)
            m = (run[h] + pre[b, h]).astype(BF16)
            a = al[rb, at] + jnp.dot(qb[rb, at], m, preferred_element_type=F32)
            a = a * lax.rsqrt(jnp.mean(a * a, axis=-1, keepdims=True) + 1e-06)
            g = hgain[:, pl.ds(pl.multiple_of(x * 256 + h * 128, 128), 128)]
            put(rb, at, (a * g).astype(BF16))

    def zero_run():
        run[...] = jnp.zeros_like(run)

    for d in (1, 3, 2):
        for p in range(3):
            start("A", d, p)
    for c in loads[:3]:
        c.wait()
    for d in SIDES:
        start("B", 0, d)
    loads[3].wait()
    loads[6].wait()
    norm_first(x)
    for e in (1, 3):
        for p in range(3):
            got("A", e, p)
        for d in SIDES:
            start("B", e, d)
    for d, h in ((1, 0), (3, 1), (1, 1), (3, 0)):
        start("C", d, h)
    for p in range(3):
        got("A", 2, p)
    for d in SIDES:
        start("B", 2, d)

    def forward_w(e):
        fd = 1 if e in (0, 3) else 3
        got("B", e, fd)
        start("F", e)

    forward_w(0)
    forward_w(1)
    got("C", 1, 0)
    start("CF", 1)
    got("C", 3, 1)
    start("CF", 3)
    forward_w(3)
    forward_w(2)
    got("C", 1, 1)
    norm_first(xr(3))
    got("C", 3, 0)
    norm_first(xr(1))
    for e in range(4):
        got("B", e, 3 if e in (0, 3) else 1)
    got("CF", 1)
    got("CF", 3)
    loads[4].wait()
    for d, h in ((1, 0), (3, 1), (1, 1), (3, 0)):
        start("D", d, h)
    for d in SIDES:
        start("K", 0, d)
    norm_first(xr(2))
    project_slice(y, True)
    project_slice(yr(3), False)
    project_slice(yr(1), False)
    for e in range(4):
        got("F", e)
    project_slice(yr(2), False)

    zero_run()
    for b in range(4):
        states(b)
    send_totals(0)
    got("D", 1, 0)
    start("DF", 1)
    got("D", 3, 1)
    start("DF", 3)
    got("D", 1, 1)
    for d in SIDES:
        start("K", 1, d)
    got("D", 3, 0)
    for d in SIDES:
        start("K", 3, d)

    def forward_k(e):
        got("K", e, 1 if e in (0, 3) else 3)
        start("KF", e)

    forward_k(0)

    @pl.when(s == 0)
    def _():
        own_fresh.start()
        for d in (1, 3, 2):
            start("R", d)

    for b in range(4):
        local(b)
    loads[5].wait()
    loads[7].wait()
    base_of(0)

    def put_first(rb, at, v):
        ho[x, rb, at] = v

    for b in range(4):
        finish(b, put_first)
        for d in SIDES:
            start("H", b, d)
    got("DF", 1)
    got("DF", 3)
    for d in SIDES:
        start("K", 2, d)
    for e in (1, 3, 2):
        forward_k(e)
    for c in range(1, 4):
        for d, h in ((1, 0), (3, 1), (1, 1), (3, 0)):
            start("E", c, d, h)

    def forward_h(b):
        got("H", b, 1)
        got("H", b, 3)
        start("HF", b)

    def out_first(b):
        got("HF", b)
        rb = pl.ds(b * 128, 128)
        for n in range(2):
            at = pl.ds(pl.multiple_of(x * 512 + n * 256, 256), 256)
            v = x1[b, :, at].astype(F32)
            for j in range(4):
                w = wof[pl.ds(4 * j, 4), :, at].reshape(256, 256)
                v += jnp.dot(ho[j, rb, :], w, preferred_element_type=F32)
            yb[rb, pl.ds(n * 256, 256)] = v.astype(BF16)

        @pl.when(s < last)
        def _():
            start("Z", b)

    def gather_second(b):
        @pl.when(s > 0)
        def _():
            got("Z", b)

        for d in SIDES:
            start("G", b, d)

    def forward_g(b):
        got("G", b, 1)
        got("G", b, 3)
        start("GF", b)

    def second(b):
        got("GF", b)
        norm_second(b)
        project_block(b)
        states(b)

    @pl.when(s == 0)
    def _():
        own_fresh.wait()
        for d in (1, 3, 2):
            got("R", d)

    forward_h(0)
    forward_h(1)
    for e in range(4):
        got("K", e, 3 if e in (0, 3) else 1)
        got("KF", e)
    out_first(0)
    forward_h(2)
    out_first(1)
    gather_second(0)
    forward_h(3)
    out_first(2)
    gather_second(1)
    out_first(3)
    forward_g(0)
    gather_second(2)
    gather_second(3)
    for c in range(1, 4):
        got("E", c, 1, 0)
        start("EF", c, 1)
        got("E", c, 3, 1)
        start("EF", c, 3)
    forward_g(1)
    zero_run()
    second(0)
    forward_g(2)
    second(1)
    forward_g(3)
    second(2)
    second(3)

    send_totals(1)
    for b in range(4):
        local(b)
    base_of(1)
    fstate[pl.ds(2 * x, 2)] = st[...].astype(BF16)

    def put_second(rb, at, v):
        ho2s[rb, at] = v

    for d in (2, 1, 3):
        finish(xr(d), put_second)
        start("H2", d)
    for d in (2, 1, 3):
        start("S", d)

    def put_own(rb, at, v):
        ho2[x, :, at] = v

    finish(x, put_own)
    for c in range(1, 4):
        got("E", c, 1, 1)
        got("E", c, 3, 0)
        got("EF", c, 1)
        got("EF", c, 3)
    for d in (1, 3, 2):
        got("H2", d)
    for n in range(8):
        at = pl.ds(n * 256, 256)
        v = x2[n // 2, rows(x), pl.ds((n % 2) * 256, 256)].astype(F32)
        for j in range(4):
            w = wof[pl.ds(4 * j, 4), :, at].reshape(256, 256)
            v += jnp.dot(ho2[j], w, preferred_element_type=F32)
        out[:, at] = v.astype(BF16)
    for d in (1, 3, 2):
        got("S", d)

    for key in IDS:
        if key[0] == "Z":
            @pl.when(s < last)
            def _():
                sent(*key)
        elif key[0] == "R":
            @pl.when(s == 0)
            def _():
                sent(*key)
        else:
            sent(*key)


def body(section_inputs, fresh_group, resident_state, qkv_weight, out_weight, input_gain, head_gain):
    anywhere = pl.BlockSpec(memory_space=pl.ANY)
    vmem = pl.BlockSpec(memory_space=pltpu.VMEM)
    n = len(IDS)
    out, state = pl.pallas_call(
        functools.partial(kernel, lax.axis_size("section") - 1),
        name="two_ticks",
        out_shape=(
            jax.ShapeDtypeStruct((128, 2048), BF16),
            jax.ShapeDtypeStruct((8, 128, 128), BF16),
        ),
        in_specs=[anywhere] * 7,
        out_specs=(vmem, vmem),
        scratch_shapes=[
            pltpu.VMEM((16, 128, 768), BF16),
            pltpu.VMEM((16, 64, 2048), BF16),
            pltpu.VMEM((4, 128, 2048), BF16),
            pltpu.VMEM((4, 512, 512), BF16),
            pltpu.VMEM((4, 512, 512), BF16),
            pltpu.VMEM((512, 768), F32),
            pltpu.VMEM((512, 256), BF16),
            pltpu.VMEM((512, 256), BF16),
            pltpu.VMEM((512, 256), BF16),
            pltpu.VMEM((512, 256), F32),
            pltpu.VMEM((4, 2, 128, 128), F32),
            pltpu.VMEM((2, 128, 128), F32),
            pltpu.VMEM((2, 4, 2, 128, 128), BF16),
            pltpu.VMEM((4, 512, 256), BF16),
            pltpu.VMEM((512, 256), BF16),
            pltpu.VMEM((4, 128, 256), BF16),
            pltpu.VMEM((512, 512), BF16),
            pltpu.VMEM((2, 128, 128), F32),
            pltpu.VMEM((1, 2048), F32),
            pltpu.VMEM((1, 1024), F32),
            pltpu.SemaphoreType.DMA((n,)),
            pltpu.SemaphoreType.DMA((n,)),
            pltpu.SemaphoreType.DMA((9,)),
        ],
        compiler_params=pltpu.CompilerParams(
            collective_id=0, has_side_effects=True, vmem_limit_bytes=61 * 2**20
        ),
        cost_estimate=pl.CostEstimate(flops=4_600_000_000, bytes_accessed=4_000_000, transcendentals=0),
    )(
        section_inputs[0], fresh_group, resident_state[0], qkv_weight[0], out_weight[0], input_gain, head_gain
    )
    return (out[None], state.astype(F32)[None])


def solution(mesh):
    in_specs = (
        P("section", "row", None),
        P("row", None),
        P("section", None, None, None),
        P("section", "row", None),
        P("section", "row", None),
        P("section", None),
        P("section", None),
    )
    out_specs = (P("section", "row", None), P("section", None, None, None))
    return jax.shard_map(body, mesh=mesh, in_specs=in_specs, out_specs=out_specs, check_vma=False)
```

```python
import functools

import jax
import jax.numpy as jnp
from jax import lax
from jax.experimental import pallas as pl
from jax.experimental.pallas import tpu as pltpu
from jax.sharding import PartitionSpec as P

MESH = pl.DeviceIdType.MESH
F32 = jnp.float32
BF16 = jnp.bfloat16
SIDES = (1, 3)
IDS = {}


def slot(*key):
    return IDS.setdefault(key, len(IDS))


for _d in (1, 3, 2):
    for _p in range(3):
        slot("A", _d, _p)
for _e in range(4):
    slot("B", _e, 1), slot("B", _e, 3), slot("F", _e)
    slot("K", _e, 1), slot("K", _e, 3), slot("KF", _e)
for _d in SIDES:
    for _h in range(2):
        slot("C", _d, _h), slot("D", _d, _h)
        for _c in range(1, 4):
            slot("E", _c, _d, _h)
    slot("CF", _d), slot("DF", _d)
    for _c in range(1, 4):
        slot("EF", _c, _d)
for _b in range(4):
    for _d in SIDES:
        slot("H", _b, _d), slot("G", _b, _d)
    slot("HF", _b), slot("GF", _b), slot("Z", _b)
for _d in (1, 2, 3):
    slot("T", 0, _d), slot("T", 1, _d), slot("R", _d), slot("H2", _d), slot("S", _d), slot("U", _d)


def kernel(
    last, x_in, fresh, state_in, w_in, wo_in, gain_in, hgain_in, out, fstate,
    wb, wof, x1, x2, nb, pj, qb, kb, vb, al, pre, run, tsum, ho, ho2s, ho2, yb, st, gain, hgain,
    ss, rs, ls,
):
    s = lax.axis_index("section")
    r = lax.axis_index("row")
    y = r // 4
    x = lax.rem(r, 4)

    def xr(d):
        return lax.rem(x + d, 4)

    def yr(d):
        return lax.rem(y + d, 4)

    def dx(d):
        return (s, y * 4 + xr(d))

    def dy(d):
        return (s, yr(d) * 4 + x)

    def rows(b):
        return pl.ds(pl.multiple_of(b * 128, 128), 128)

    def cols(j, n):
        return pl.ds(pl.multiple_of(j * n, n), n)

    quarter = pl.ds(pl.multiple_of(32 * y, 32), 32)
    makers = {}

    def define(key, src, dst, dev):
        i = IDS[key]
        makers[key] = lambda: pltpu.make_async_remote_copy(
            src_ref=src, dst_ref=dst, send_sem=ss.at[i], recv_sem=rs.at[i],
            device_id=dev, device_id_type=MESH,
        )

    def start(*key):
        makers[key]().start()

    def got(*key):
        makers[key]().wait_recv()

    def sent(*key):
        makers[key]().wait_send()

    for d in (1, 3, 2):
        for p in range(3):
            define(("A", d, p), w_in.at[:, pl.ds(pl.multiple_of(p * 1024 + xr(d) * 256, 256), 256)],
                   wb.at[r, :, pl.ds(p * 256, 256)], dx(d))
    for e in range(4):
        k = y * 4 + xr(4 - e)
        for d in SIDES:
            define(("B", e, d), wb.at[k], wb.at[k], dy(d))
        fd = 1 if e in (0, 3) else 3
        k2 = yr(4 - fd) * 4 + xr(4 - e)
        define(("F", e), wb.at[k2], wb.at[k2], dy(fd))
        for d in SIDES:
            v = wof.at[k, :, cols(x, 512)]
            define(("K", e, d), v, v, dy(d))
        v = wof.at[k2, :, cols(x, 512)]
        define(("KF", e), v, v, dy(fd))
    for d in SIDES:
        for h in range(2):
            v = x1.at[x, pl.ds(h * 64, 64)]
            define(("C", d, h), v, v, dx(d))
            v = wof.at[r, pl.ds(h * 32, 32)]
            define(("D", d, h), v, v, dx(d))
        h = 0 if d == 1 else 1
        v = x1.at[xr(4 - d), pl.ds(h * 64, 64)]
        define(("CF", d), v, v, dx(d))
        v = wof.at[y * 4 + xr(4 - d), pl.ds(h * 32, 32)]
        define(("DF", d), v, v, dx(d))
    for c in range(1, 4):
        for d in SIDES:
            for h in range(2):
                v = wof.at[pl.ds(y * 4 + 2 * h, 2), :, cols(xr(c), 512)]
                define(("E", c, d, h), v, v, dy(d))
            h = 0 if d == 1 else 1
            v = wof.at[pl.ds(yr(4 - d) * 4 + 2 * h, 2), :, cols(xr(c), 512)]
            define(("EF", c, d), v, v, dy(d))
    for d in (1, 2, 3):
        for t in range(2):
            define(("T", t, d), tsum.at[t, y], tsum.at[t, y], dy(d))
        define(("R", d), fresh.at[:, cols(xr(d), 512)], x2.at[xr(d), rows(x)], dx(d))
        define(("H2", d), ho2s.at[rows(xr(d))], ho2.at[x], dx(d))
        v = fstate.at[pl.ds(2 * x, 2), quarter]
        define(("S", d), v, v, dx(d))
        v = fstate.at[:, quarter]
        define(("U", d), v, v, dy(d))
    for b in range(4):
        rb = pl.ds(b * 128, 128)
        for d in SIDES:
            v = ho.at[x, rb]
            define(("H", b, d), v, v, dx(d))
            v = x2.at[x, rb]
            define(("G", b, d), v, v, dx(d))
        fd = 1 if b % 2 == 0 else 3
        v = ho.at[xr(4 - fd), rb]
        define(("HF", b), v, v, dx(fd))
        v = x2.at[xr(4 - fd), rb]
        define(("GF", b), v, v, dx(fd))
        define(("Z", b), yb.at[rb], x2.at[x, rb], (s + 1, r))

    loads = [
        pltpu.make_async_copy(w_in.at[:, pl.ds(pl.multiple_of(p * 1024 + x * 256, 256), 256)],
                              wb.at[r, :, pl.ds(p * 256, 256)], ls.at[p])
        for p in range(3)
    ]
    loads.append(pltpu.make_async_copy(x_in, x1.at[x], ls.at[3]))
    loads.append(pltpu.make_async_copy(wo_in, wof.at[r], ls.at[4]))
    loads.append(pltpu.make_async_copy(state_in.at[pl.ds(2 * x, 2)], st, ls.at[5]))
    loads.append(pltpu.make_async_copy(gain_in, gain, ls.at[6]))
    loads.append(pltpu.make_async_copy(hgain_in, hgain, ls.at[7]))
    for c in loads:
        c.start()
    own_fresh = pltpu.make_async_copy(fresh.at[:, cols(x, 512)], x2.at[x, rows(x)], ls.at[8])

    barrier = pltpu.get_barrier_semaphore()
    before, after = (lax.rem(s + last, last + 1), r), (lax.rem(s + 1, last + 1), r)
    for dev in [dx(1), dx(2), dx(3), dy(1), dy(2), dy(3), before, after]:
        pl.semaphore_signal(barrier, inc=1, device_id=dev, device_id_type=MESH)
    pl.semaphore_wait(barrier, 8)

    def norm_first(b):
        def strip(i, carry):
            at = pl.ds(pl.multiple_of(i * 16, 16), 16)
            v = x1[b, at, :].astype(F32)
            scale = lax.rsqrt(jnp.mean(v * v, axis=-1, keepdims=True) + 1e-05)
            n = (v * scale * gain[...]).astype(BF16)
            to = pl.ds(pl.multiple_of(b * 128 + i * 16, 16), 16)
            for p in range(4):
                nb[p, to, :] = n[:, p * 512:(p + 1) * 512]
            return carry
        lax.fori_loop(0, 8, strip, 0, unroll=4)

    def norm_second(b):
        def strip(i, carry):
            at = pl.ds(pl.multiple_of(b * 128 + i * 16, 16), 16)
            v = [x2[p, at, :].astype(F32) for p in range(4)]
            sq = sum(jnp.sum(u * u, axis=-1, keepdims=True) for u in v)
            scale = lax.rsqrt(sq * (1.0 / 2048) + 1e-05)
            for p in range(4):
                nb[p, at, :] = (v[p] * scale * gain[:, p * 512:(p + 1) * 512]).astype(BF16)
            return carry
        lax.fori_loop(0, 8, strip, 0, unroll=4)

    def project_slice(kg, first):
        for n in range(3):
            at = pl.ds(n * 256, 256)
            w = wb[pl.ds(4 * kg, 4), :, at].reshape(512, 256)
            v = jnp.dot(nb[kg], w, preferred_element_type=F32)
            if first:
                pj[:, at] = v
            else:
                pj[:, at] += v

    def project_block(b):
        rb = pl.ds(b * 128, 128)
        for n in range(3):
            at = pl.ds(n * 256, 256)
            v = jnp.zeros((128, 256), F32)
            for kg in range(4):
                w = wb[pl.ds(4 * kg, 4), :, at].reshape(512, 256)
                v += jnp.dot(nb[kg, rb, :], w, preferred_element_type=F32)
            pj[rb, at] = v

    def states(b):
        rb = rows(b)
        for h in range(2):
            at = pl.ds(h * 128, 128)
            q = pj[rb, pl.ds(h * 128, 128)]
            qb[rb, at] = (q / (1.0 + jnp.exp(-q))).astype(BF16)
            k = pj[rb, pl.ds(256 + h * 128, 128)]
            k = (k / (1.0 + jnp.exp(-k))).astype(BF16)
            kb[rb, at] = k
            v = pj[rb, pl.ds(512 + h * 128, 128)].astype(BF16)
            vb[rb, at] = v
            pre[b, h] = run[h]
            run[h] += lax.dot_general(k, v, (((0,), (0,)), ((), ())), preferred_element_type=F32)

    def local(b):
        rb = rows(b)
        keep = lax.broadcasted_iota(jnp.int32, (128, 128), 0) >= lax.broadcasted_iota(jnp.int32, (128, 128), 1)
        for h in range(2):
            at = pl.ds(h * 128, 128)
            sc = lax.dot_general(qb[rb, at], kb[rb, at], (((1,), (1,)), ((), ())), preferred_element_type=F32)
            w = jnp.where(keep, sc, 0.0).astype(BF16)
            al[rb, at] = jnp.dot(w, vb[rb, at], preferred_element_type=F32)

    def send_totals(t):
        tsum[t, y] = run[...].astype(BF16)
        for d in (1, 3, 2):
            start("T", t, d)

    def base_of(t):
        for d in (1, 3, 2):
            got("T", t, d)
        before = st[...]
        total = st[...]
        for i in range(4):
            u = tsum[t, i].astype(F32)
            before = before + u * (y > i).astype(F32)
            total = total + u
        run[...] = before
        st[...] = total

    def finish(b, put):
        rb = rows(b)
        for h in range(2):
            at = pl.ds(h * 128, 128)
            m = (run[h] + pre[b, h]).astype(BF16)
            a = al[rb, at] + jnp.dot(qb[rb, at], m, preferred_element_type=F32)
            a = a * lax.rsqrt(jnp.mean(a * a, axis=-1, keepdims=True) + 1e-06)
            g = hgain[:, pl.ds(pl.multiple_of(x * 256 + h * 128, 128), 128)]
            put(rb, at, (a * g).astype(BF16))

    def zero_run():
        run[...] = jnp.zeros_like(run)

    for d in (1, 3, 2):
        for p in range(3):
            start("A", d, p)
    for c in loads[:3]:
        c.wait()
    for d in SIDES:
        start("B", 0, d)
    loads[3].wait()
    loads[6].wait()
    norm_first(x)
    for e in (1, 3):
        for p in range(3):
            got("A", e, p)
        for d in SIDES:
            start("B", e, d)
    for d, h in ((1, 0), (3, 1), (1, 1), (3, 0)):
        start("C", d, h)
    for p in range(3):
        got("A", 2, p)
    for d in SIDES:
        start("B", 2, d)

    def forward_w(e):
        fd = 1 if e in (0, 3) else 3
        got("B", e, fd)
        start("F", e)

    forward_w(0)
    forward_w(1)
    got("C", 1, 0)
    start("CF", 1)
    got("C", 3, 1)
    start("CF", 3)
    forward_w(3)
    forward_w(2)
    got("C", 1, 1)
    norm_first(xr(3))
    got("C", 3, 0)
    norm_first(xr(1))
    for e in range(4):
        got("B", e, 3 if e in (0, 3) else 1)
    got("CF", 1)
    got("CF", 3)
    loads[4].wait()
    for d, h in ((1, 0), (3, 1), (1, 1), (3, 0)):
        start("D", d, h)
    for d in SIDES:
        start("K", 0, d)
    norm_first(xr(2))
    project_slice(y, True)
    project_slice(yr(3), False)
    project_slice(yr(1), False)
    for e in range(4):
        got("F", e)
    project_slice(yr(2), False)

    zero_run()
    for b in range(4):
        states(b)
    send_totals(0)
    got("D", 1, 0)
    start("DF", 1)
    got("D", 3, 1)
    start("DF", 3)
    got("D", 1, 1)
    for d in SIDES:
        start("K", 1, d)
    got("D", 3, 0)
    for d in SIDES:
        start("K", 3, d)

    def forward_k(e):
        got("K", e, 1 if e in (0, 3) else 3)
        start("KF", e)

    forward_k(0)

    @pl.when(s == 0)
    def _():
        own_fresh.start()
        for d in (1, 3, 2):
            start("R", d)

    for b in range(4):
        local(b)
    loads[5].wait()
    loads[7].wait()
    base_of(0)

    def put_first(rb, at, v):
        ho[x, rb, at] = v

    for b in range(4):
        finish(b, put_first)
        for d in SIDES:
            start("H", b, d)
    got("DF", 1)
    got("DF", 3)
    for d in SIDES:
        start("K", 2, d)
    for e in (1, 3, 2):
        forward_k(e)
    for c in range(1, 4):
        for d, h in ((1, 0), (3, 1), (1, 1), (3, 0)):
            start("E", c, d, h)

    def forward_h(b):
        got("H", b, 1)
        got("H", b, 3)
        start("HF", b)

    def out_first(b):
        got("HF", b)
        rb = pl.ds(b * 128, 128)
        for n in range(2):
            at = pl.ds(pl.multiple_of(x * 512 + n * 256, 256), 256)
            v = x1[b, :, at].astype(F32)
            for j in range(4):
                w = wof[pl.ds(4 * j, 4), :, at].reshape(256, 256)
                v += jnp.dot(ho[j, rb, :], w, preferred_element_type=F32)
            yb[rb, pl.ds(n * 256, 256)] = v.astype(BF16)

        @pl.when(s < last)
        def _():
            start("Z", b)

    def gather_second(b):
        @pl.when(s > 0)
        def _():
            got("Z", b)

        for d in SIDES:
            start("G", b, d)

    def forward_g(b):
        got("G", b, 1)
        got("G", b, 3)
        start("GF", b)

    def second(b):
        got("GF", b)
        norm_second(b)
        project_block(b)
        states(b)

    @pl.when(s == 0)
    def _():
        own_fresh.wait()
        for d in (1, 3, 2):
            got("R", d)

    forward_h(0)
    forward_h(1)
    for e in range(4):
        got("K", e, 3 if e in (0, 3) else 1)
        got("KF", e)
    out_first(0)
    forward_h(2)
    out_first(1)
    gather_second(0)
    forward_h(3)
    out_first(2)
    gather_second(1)
    out_first(3)
    forward_g(0)
    gather_second(2)
    gather_second(3)
    for c in range(1, 4):
        got("E", c, 1, 0)
        start("EF", c, 1)
        got("E", c, 3, 1)
        start("EF", c, 3)
    forward_g(1)
    zero_run()
    second(0)
    forward_g(2)
    second(1)
    forward_g(3)
    second(2)
    second(3)

    send_totals(1)
    for b in range(4):
        local(b)
    base_of(1)
    fstate[pl.ds(2 * x, 2), quarter] = st[:, quarter].astype(BF16)
    for d in (2, 1, 3):
        start("S", d)

    def put_second(rb, at, v):
        ho2s[rb, at] = v

    for d in (2, 1, 3):
        finish(xr(d), put_second)
        start("H2", d)

    def put_own(rb, at, v):
        ho2[x, :, at] = v

    for d in (2, 1, 3):
        got("S", d)
    for d in (2, 1, 3):
        start("U", d)
    finish(x, put_own)
    for c in range(1, 4):
        got("E", c, 1, 1)
        got("E", c, 3, 0)
        got("EF", c, 1)
        got("EF", c, 3)
    for d in (1, 3, 2):
        got("H2", d)
    for n in range(8):
        at = pl.ds(n * 256, 256)
        v = x2[n // 2, rows(x), pl.ds((n % 2) * 256, 256)].astype(F32)
        for j in range(4):
            w = wof[pl.ds(4 * j, 4), :, at].reshape(256, 256)
            v += jnp.dot(ho2[j], w, preferred_element_type=F32)
        out[:, at] = v.astype(BF16)
    for d in (1, 3, 2):
        got("U", d)

    for key in IDS:
        if key[0] == "Z":
            @pl.when(s < last)
            def _():
                sent(*key)
        elif key[0] == "R":
            @pl.when(s == 0)
            def _():
                sent(*key)
        else:
            sent(*key)


def body(section_inputs, fresh_group, resident_state, qkv_weight, out_weight, input_gain, head_gain):
    anywhere = pl.BlockSpec(memory_space=pl.ANY)
    vmem = pl.BlockSpec(memory_space=pltpu.VMEM)
    n = len(IDS)
    out, state = pl.pallas_call(
        functools.partial(kernel, lax.axis_size("section") - 1),
        name="two_ticks",
        out_shape=(
            jax.ShapeDtypeStruct((128, 2048), BF16),
            jax.ShapeDtypeStruct((8, 128, 128), BF16),
        ),
        in_specs=[anywhere] * 7,
        out_specs=(vmem, vmem),
        scratch_shapes=[
            pltpu.VMEM((16, 128, 768), BF16),
            pltpu.VMEM((16, 64, 2048), BF16),
            pltpu.VMEM((4, 128, 2048), BF16),
            pltpu.VMEM((4, 512, 512), BF16),
            pltpu.VMEM((4, 512, 512), BF16),
            pltpu.VMEM((512, 768), F32),
            pltpu.VMEM((512, 256), BF16),
            pltpu.VMEM((512, 256), BF16),
            pltpu.VMEM((512, 256), BF16),
            pltpu.VMEM((512, 256), F32),
            pltpu.VMEM((4, 2, 128, 128), F32),
            pltpu.VMEM((2, 128, 128), F32),
            pltpu.VMEM((2, 4, 2, 128, 128), BF16),
            pltpu.VMEM((4, 512, 256), BF16),
            pltpu.VMEM((512, 256), BF16),
            pltpu.VMEM((4, 128, 256), BF16),
            pltpu.VMEM((512, 512), BF16),
            pltpu.VMEM((2, 128, 128), F32),
            pltpu.VMEM((1, 2048), F32),
            pltpu.VMEM((1, 1024), F32),
            pltpu.SemaphoreType.DMA((n,)),
            pltpu.SemaphoreType.DMA((n,)),
            pltpu.SemaphoreType.DMA((9,)),
        ],
        compiler_params=pltpu.CompilerParams(
            collective_id=0, has_side_effects=True, vmem_limit_bytes=61 * 2**20
        ),
        cost_estimate=pl.CostEstimate(flops=4_600_000_000, bytes_accessed=4_000_000, transcendentals=0),
    )(
        section_inputs[0], fresh_group, resident_state[0], qkv_weight[0], out_weight[0], input_gain, head_gain
    )
    return (out[None], state.astype(F32)[None])


def solution(mesh):
    in_specs = (
        P("section", "row", None),
        P("row", None),
        P("section", None, None, None),
        P("section", "row", None),
        P("section", "row", None),
        P("section", None),
        P("section", None),
    )
    out_specs = (P("section", "row", None), P("section", None, None, None))
    return jax.shard_map(body, mesh=mesh, in_specs=in_specs, out_specs=out_specs, check_vma=False)
```

```python
import functools

import jax
import jax.numpy as jnp
from jax import lax
from jax.experimental import pallas as pl
from jax.experimental.pallas import tpu as pltpu
from jax.sharding import PartitionSpec as P

MESH = pl.DeviceIdType.MESH
F32 = jnp.float32
BF16 = jnp.bfloat16
SIDES = (1, 3)
IDS = {}


def slot(*key):
    return IDS.setdefault(key, len(IDS))


for _d in (1, 3, 2):
    for _p in range(3):
        slot("A", _d, _p)
for _e in range(4):
    slot("B", _e, 1), slot("B", _e, 3), slot("F", _e)
    slot("K", _e, 1), slot("K", _e, 3), slot("KF", _e)
for _d in SIDES:
    for _h in range(2):
        slot("C", _d, _h), slot("D", _d, _h)
        for _c in range(1, 4):
            slot("E", _c, _d, _h)
    slot("CF", _d), slot("DF", _d)
    for _c in range(1, 4):
        slot("EF", _c, _d)
for _b in range(4):
    for _d in SIDES:
        slot("H", _b, _d), slot("G", _b, _d)
    slot("HF", _b), slot("GF", _b), slot("Z", _b)
for _d in (1, 2, 3):
    slot("T", 0, _d), slot("T", 1, _d), slot("R", _d), slot("H2", _d), slot("S", _d)


def kernel(
    last, x_in, fresh, state_in, w_in, wo_in, gain_in, hgain_in, out, fstate,
    wb, wof, x1, x2, nb, pj, qb, kb, vb, al, pre, run, tsum, ho, ho2s, ho2, yb, st, gain, hgain,
    ss, rs, ls,
):
    s = lax.axis_index("section")
    r = lax.axis_index("row")
    y = r // 4
    x = lax.rem(r, 4)

    def xr(d):
        return lax.rem(x + d, 4)

    def yr(d):
        return lax.rem(y + d, 4)

    def dx(d):
        return (s, y * 4 + xr(d))

    def dy(d):
        return (s, yr(d) * 4 + x)

    def rows(b):
        return pl.ds(pl.multiple_of(b * 128, 128), 128)

    def cols(j, n):
        return pl.ds(pl.multiple_of(j * n, n), n)

    makers = {}

    def define(key, src, dst, dev):
        i = IDS[key]
        makers[key] = lambda: pltpu.make_async_remote_copy(
            src_ref=src, dst_ref=dst, send_sem=ss.at[i], recv_sem=rs.at[i],
            device_id=dev, device_id_type=MESH,
        )

    def start(*key):
        makers[key]().start()

    def got(*key):
        makers[key]().wait_recv()

    def sent(*key):
        makers[key]().wait_send()

    for d in (1, 3, 2):
        for p in range(3):
            define(("A", d, p), w_in.at[:, pl.ds(pl.multiple_of(p * 1024 + xr(d) * 256, 256), 256)],
                   wb.at[r, :, pl.ds(p * 256, 256)], dx(d))
    for e in range(4):
        k = y * 4 + xr(4 - e)
        for d in SIDES:
            define(("B", e, d), wb.at[k], wb.at[k], dy(d))
        fd = 1 if e in (0, 3) else 3
        k2 = yr(4 - fd) * 4 + xr(4 - e)
        define(("F", e), wb.at[k2], wb.at[k2], dy(fd))
        for d in SIDES:
            v = wof.at[k, :, cols(x, 512)]
            define(("K", e, d), v, v, dy(d))
        v = wof.at[k2, :, cols(x, 512)]
        define(("KF", e), v, v, dy(fd))
    for d in SIDES:
        for h in range(2):
            v = x1.at[x, pl.ds(h * 64, 64)]
            define(("C", d, h), v, v, dx(d))
            v = wof.at[r, pl.ds(h * 32, 32)]
            define(("D", d, h), v, v, dx(d))
        h = 0 if d == 1 else 1
        v = x1.at[xr(4 - d), pl.ds(h * 64, 64)]
        define(("CF", d), v, v, dx(d))
        v = wof.at[y * 4 + xr(4 - d), pl.ds(h * 32, 32)]
        define(("DF", d), v, v, dx(d))
    for c in range(1, 4):
        for d in SIDES:
            for h in range(2):
                v = wof.at[pl.ds(y * 4 + 2 * h, 2), :, cols(xr(c), 512)]
                define(("E", c, d, h), v, v, dy(d))
            h = 0 if d == 1 else 1
            v = wof.at[pl.ds(yr(4 - d) * 4 + 2 * h, 2), :, cols(xr(c), 512)]
            define(("EF", c, d), v, v, dy(d))
    for d in (1, 2, 3):
        for t in range(2):
            define(("T", t, d), tsum.at[t, y], tsum.at[t, y], dy(d))
        define(("R", d), fresh.at[:, cols(xr(d), 512)], x2.at[xr(d), rows(x)], dx(d))
        define(("H2", d), ho2s.at[rows(xr(d))], ho2.at[x], dx(d))
        define(("S", d), fstate.at[pl.ds(2 * x, 2)], fstate.at[pl.ds(2 * x, 2)], dx(d))
    for b in range(4):
        rb = pl.ds(b * 128, 128)
        for d in SIDES:
            v = ho.at[x, rb]
            define(("H", b, d), v, v, dx(d))
            v = x2.at[x, rb]
            define(("G", b, d), v, v, dx(d))
        fd = 1 if b % 2 == 0 else 3
        v = ho.at[xr(4 - fd), rb]
        define(("HF", b), v, v, dx(fd))
        v = x2.at[xr(4 - fd), rb]
        define(("GF", b), v, v, dx(fd))
        define(("Z", b), yb.at[rb], x2.at[x, rb], (s + 1, r))

    loads = [
        pltpu.make_async_copy(w_in.at[:, pl.ds(pl.multiple_of(p * 1024 + x * 256, 256), 256)],
                              wb.at[r, :, pl.ds(p * 256, 256)], ls.at[p])
        for p in range(3)
    ]
    loads.append(pltpu.make_async_copy(x_in, x1.at[x], ls.at[3]))
    loads.append(pltpu.make_async_copy(wo_in, wof.at[r], ls.at[4]))
    loads.append(pltpu.make_async_copy(state_in.at[pl.ds(2 * x, 2)], st, ls.at[5]))
    loads.append(pltpu.make_async_copy(gain_in, gain, ls.at[6]))
    loads.append(pltpu.make_async_copy(hgain_in, hgain, ls.at[7]))
    for c in loads:
        c.start()
    own_fresh = pltpu.make_async_copy(fresh.at[:, cols(x, 512)], x2.at[x, rows(x)], ls.at[8])

    barrier = pltpu.get_barrier_semaphore()
    before, after = (lax.rem(s + last, last + 1), r), (lax.rem(s + 1, last + 1), r)
    for dev in [dx(1), dx(2), dx(3), dy(1), dy(2), dy(3), before, after]:
        pl.semaphore_signal(barrier, inc=1, device_id=dev, device_id_type=MESH)
    pl.semaphore_wait(barrier, 8)

    def norm_first(b):
        def strip(i, carry):
            at = pl.ds(pl.multiple_of(i * 16, 16), 16)
            v = x1[b, at, :].astype(F32)
            scale = lax.rsqrt(jnp.mean(v * v, axis=-1, keepdims=True) + 1e-05)
            n = (v * scale * gain[...]).astype(BF16)
            to = pl.ds(pl.multiple_of(b * 128 + i * 16, 16), 16)
            for p in range(4):
                nb[p, to, :] = n[:, p * 512:(p + 1) * 512]
            return carry
        lax.fori_loop(0, 8, strip, 0, unroll=4)

    def norm_second(b):
        def strip(i, carry):
            at = pl.ds(pl.multiple_of(b * 128 + i * 16, 16), 16)
            v = [x2[p, at, :].astype(F32) for p in range(4)]
            sq = sum(jnp.sum(u * u, axis=-1, keepdims=True) for u in v)
            scale = lax.rsqrt(sq * (1.0 / 2048) + 1e-05)
            for p in range(4):
                nb[p, at, :] = (v[p] * scale * gain[:, p * 512:(p + 1) * 512]).astype(BF16)
            return carry
        lax.fori_loop(0, 8, strip, 0, unroll=4)

    def project_slice(kg, first):
        for n in range(3):
            at = pl.ds(n * 256, 256)
            w = wb[pl.ds(4 * kg, 4), :, at].reshape(512, 256)
            v = jnp.dot(nb[kg], w, preferred_element_type=F32)
            if first:
                pj[:, at] = v
            else:
                pj[:, at] += v

    def project_block(b):
        rb = pl.ds(b * 128, 128)
        for n in range(3):
            at = pl.ds(n * 256, 256)
            v = jnp.zeros((128, 256), F32)
            for kg in range(4):
                w = wb[pl.ds(4 * kg, 4), :, at].reshape(512, 256)
                v += jnp.dot(nb[kg, rb, :], w, preferred_element_type=F32)
            pj[rb, at] = v

    def states(b):
        rb = rows(b)
        for h in range(2):
            at = pl.ds(h * 128, 128)
            q = pj[rb, pl.ds(h * 128, 128)]
            qb[rb, at] = (q / (1.0 + jnp.exp(-q))).astype(BF16)
            k = pj[rb, pl.ds(256 + h * 128, 128)]
            k = (k / (1.0 + jnp.exp(-k))).astype(BF16)
            kb[rb, at] = k
            v = pj[rb, pl.ds(512 + h * 128, 128)].astype(BF16)
            vb[rb, at] = v
            pre[b, h] = run[h]
            run[h] += lax.dot_general(k, v, (((0,), (0,)), ((), ())), preferred_element_type=F32)

    def local(b):
        rb = rows(b)
        keep = lax.broadcasted_iota(jnp.int32, (128, 128), 0) >= lax.broadcasted_iota(jnp.int32, (128, 128), 1)
        for h in range(2):
            at = pl.ds(h * 128, 128)
            sc = lax.dot_general(qb[rb, at], kb[rb, at], (((1,), (1,)), ((), ())), preferred_element_type=F32)
            w = jnp.where(keep, sc, 0.0).astype(BF16)
            al[rb, at] = jnp.dot(w, vb[rb, at], preferred_element_type=F32)

    def send_totals(t):
        tsum[t, y] = run[...].astype(BF16)
        for d in (1, 3, 2):
            start("T", t, d)

    def base_of(t):
        for d in (1, 3, 2):
            got("T", t, d)
        before = st[...]
        total = st[...]
        for i in range(4):
            u = tsum[t, i].astype(F32)
            before = before + u * (y > i).astype(F32)
            total = total + u
        run[...] = before
        st[...] = total

    def finish(b, put):
        rb = rows(b)
        for h in range(2):
            at = pl.ds(h * 128, 128)
            m = (run[h] + pre[b, h]).astype(BF16)
            a = al[rb, at] + jnp.dot(qb[rb, at], m, preferred_element_type=F32)
            a = a * lax.rsqrt(jnp.mean(a * a, axis=-1, keepdims=True) + 1e-06)
            g = hgain[:, pl.ds(pl.multiple_of(x * 256 + h * 128, 128), 128)]
            put(rb, at, (a * g).astype(BF16))

    def zero_run():
        run[...] = jnp.zeros_like(run)

    for d in (1, 3, 2):
        for p in range(3):
            start("A", d, p)
    for c in loads[:3]:
        c.wait()
    for d in SIDES:
        start("B", 0, d)
    loads[3].wait()
    loads[6].wait()
    norm_first(x)
    for e in (1, 3):
        for p in range(3):
            got("A", e, p)
        for d in SIDES:
            start("B", e, d)
    for d, h in ((1, 0), (3, 1), (1, 1), (3, 0)):
        start("C", d, h)
    for p in range(3):
        got("A", 2, p)
    for d in SIDES:
        start("B", 2, d)

    def forward_w(e):
        fd = 1 if e in (0, 3) else 3
        got("B", e, fd)
        start("F", e)

    forward_w(0)
    forward_w(1)
    got("C", 1, 0)
    start("CF", 1)
    got("C", 3, 1)
    start("CF", 3)
    forward_w(3)
    forward_w(2)
    got("C", 1, 1)
    norm_first(xr(3))
    got("C", 3, 0)
    loads[4].wait()
    for d, h in ((1, 0), (3, 1), (1, 1), (3, 0)):
        start("D", d, h)
    for d in SIDES:
        start("K", 0, d)
    norm_first(xr(1))
    for e in range(4):
        got("B", e, 3 if e in (0, 3) else 1)
    got("CF", 1)
    got("CF", 3)
    norm_first(xr(2))
    project_slice(y, True)
    project_slice(yr(3), False)
    project_slice(yr(1), False)
    for e in range(4):
        got("F", e)
    project_slice(yr(2), False)

    zero_run()
    for b in range(4):
        states(b)
    send_totals(0)
    got("D", 1, 0)
    start("DF", 1)
    got("D", 3, 1)
    start("DF", 3)
    got("D", 1, 1)
    for d in SIDES:
        start("K", 1, d)
    got("D", 3, 0)
    for d in SIDES:
        start("K", 3, d)

    def forward_k(e):
        got("K", e, 1 if e in (0, 3) else 3)
        start("KF", e)

    forward_k(0)

    @pl.when(s == 0)
    def _():
        own_fresh.start()
        for d in (1, 3, 2):
            start("R", d)

    for b in range(4):
        local(b)
    loads[5].wait()
    loads[7].wait()
    base_of(0)

    def put_first(rb, at, v):
        ho[x, rb, at] = v

    for b in range(4):
        finish(b, put_first)
        for d in SIDES:
            start("H", b, d)
    got("DF", 1)
    got("DF", 3)
    for d in SIDES:
        start("K", 2, d)
    for e in (1, 3, 2):
        forward_k(e)
    for c in range(1, 4):
        for d, h in ((1, 0), (3, 1), (1, 1), (3, 0)):
            start("E", c, d, h)

    def forward_h(b):
        got("H", b, 1)
        got("H", b, 3)
        start("HF", b)

    def out_first(b):
        got("HF", b)
        rb = pl.ds(b * 128, 128)
        for n in range(2):
            at = pl.ds(pl.multiple_of(x * 512 + n * 256, 256), 256)
            v = x1[b, :, at].astype(F32)
            for j in range(4):
                w = wof[pl.ds(4 * j, 4), :, at].reshape(256, 256)
                v += jnp.dot(ho[j, rb, :], w, preferred_element_type=F32)
            yb[rb, pl.ds(n * 256, 256)] = v.astype(BF16)

        @pl.when(s < last)
        def _():
            start("Z", b)

    def gather_second(b):
        @pl.when(s > 0)
        def _():
            got("Z", b)

        for d in SIDES:
            start("G", b, d)

    def forward_g(b):
        got("G", b, 1)
        got("G", b, 3)
        start("GF", b)

    def second(b):
        got("GF", b)
        norm_second(b)
        project_block(b)
        states(b)

    @pl.when(s == 0)
    def _():
        own_fresh.wait()
        for d in (1, 3, 2):
            got("R", d)

    forward_h(0)
    forward_h(1)
    for e in range(4):
        got("K", e, 3 if e in (0, 3) else 1)
        got("KF", e)
    out_first(0)
    forward_h(2)
    out_first(1)
    gather_second(0)
    forward_h(3)
    out_first(2)
    gather_second(1)
    out_first(3)
    forward_g(0)
    gather_second(2)
    gather_second(3)
    for c in range(1, 4):
        got("E", c, 1, 0)
        start("EF", c, 1)
        got("E", c, 3, 1)
        start("EF", c, 3)
    forward_g(1)
    zero_run()
    second(0)
    forward_g(2)
    second(1)
    forward_g(3)
    second(2)
    second(3)

    send_totals(1)
    for b in range(4):
        local(b)
    base_of(1)
    fstate[pl.ds(2 * x, 2)] = st[...].astype(BF16)

    def put_second(rb, at, v):
        ho2s[rb, at] = v

    for d in (2, 1, 3):
        finish(xr(d), put_second)
        start("H2", d)
    for d in (2, 1, 3):
        start("S", d)

    def put_own(rb, at, v):
        ho2[x, :, at] = v

    finish(x, put_own)
    for c in range(1, 4):
        got("E", c, 1, 1)
        got("E", c, 3, 0)
        got("EF", c, 1)
        got("EF", c, 3)
    for d in (1, 3, 2):
        got("H2", d)
    for n in range(8):
        at = pl.ds(n * 256, 256)
        v = x2[n // 2, rows(x), pl.ds((n % 2) * 256, 256)].astype(F32)
        for j in range(4):
            w = wof[pl.ds(4 * j, 4), :, at].reshape(256, 256)
            v += jnp.dot(ho2[j], w, preferred_element_type=F32)
        out[:, at] = v.astype(BF16)
    for d in (1, 3, 2):
        got("S", d)

    for key in IDS:
        if key[0] == "Z":
            @pl.when(s < last)
            def _():
                sent(*key)
        elif key[0] == "R":
            @pl.when(s == 0)
            def _():
                sent(*key)
        else:
            sent(*key)


def body(section_inputs, fresh_group, resident_state, qkv_weight, out_weight, input_gain, head_gain):
    anywhere = pl.BlockSpec(memory_space=pl.ANY)
    vmem = pl.BlockSpec(memory_space=pltpu.VMEM)
    n = len(IDS)
    out, state = pl.pallas_call(
        functools.partial(kernel, lax.axis_size("section") - 1),
        name="two_ticks",
        out_shape=(
            jax.ShapeDtypeStruct((128, 2048), BF16),
            jax.ShapeDtypeStruct((8, 128, 128), BF16),
        ),
        in_specs=[anywhere] * 7,
        out_specs=(vmem, vmem),
        scratch_shapes=[
            pltpu.VMEM((16, 128, 768), BF16),
            pltpu.VMEM((16, 64, 2048), BF16),
            pltpu.VMEM((4, 128, 2048), BF16),
            pltpu.VMEM((4, 512, 512), BF16),
            pltpu.VMEM((4, 512, 512), BF16),
            pltpu.VMEM((512, 768), F32),
            pltpu.VMEM((512, 256), BF16),
            pltpu.VMEM((512, 256), BF16),
            pltpu.VMEM((512, 256), BF16),
            pltpu.VMEM((512, 256), F32),
            pltpu.VMEM((4, 2, 128, 128), F32),
            pltpu.VMEM((2, 128, 128), F32),
            pltpu.VMEM((2, 4, 2, 128, 128), BF16),
            pltpu.VMEM((4, 512, 256), BF16),
            pltpu.VMEM((512, 256), BF16),
            pltpu.VMEM((4, 128, 256), BF16),
            pltpu.VMEM((512, 512), BF16),
            pltpu.VMEM((2, 128, 128), F32),
            pltpu.VMEM((1, 2048), F32),
            pltpu.VMEM((1, 1024), F32),
            pltpu.SemaphoreType.DMA((n,)),
            pltpu.SemaphoreType.DMA((n,)),
            pltpu.SemaphoreType.DMA((9,)),
        ],
        compiler_params=pltpu.CompilerParams(
            collective_id=0, has_side_effects=True, vmem_limit_bytes=61 * 2**20
        ),
        cost_estimate=pl.CostEstimate(flops=4_600_000_000, bytes_accessed=4_000_000, transcendentals=0),
    )(
        section_inputs[0], fresh_group, resident_state[0], qkv_weight[0], out_weight[0], input_gain, head_gain
    )
    return (out[None], state.astype(F32)[None])


def solution(mesh):
    in_specs = (
        P("section", "row", None),
        P("row", None),
        P("section", None, None, None),
        P("section", "row", None),
        P("section", "row", None),
        P("section", None),
        P("section", None),
    )
    out_specs = (P("section", "row", None), P("section", None, None, None))
    return jax.shard_map(body, mesh=mesh, in_specs=in_specs, out_specs=out_specs, check_vma=False)
```
